256 devices in a mesh: wide: 32 (over z_hi, x, core), fsdp: 8 (over y, z_lo).
Axes of the slice: x: 4, y: 4, z: 8 (z_hi: 4, z_lo: 2; z = z_hi * 2 + z_lo), core: 2. Of those that a mesh axis runs over, the one named last changes fastest.
Arguments:
- tokens: bfloat16 [8192, 4096], P('wide', 'fsdp'), may hold values from -6 to 6
- norm_gain: float32 [4096], replicated, may hold values from 0.1 to 1.9
- route_ids: int32 [8192, 2], P('wide'), may hold values from 0 to 1, all different within a row
- route_gates: float32 [8192, 2], P('wide'), may hold values from 0.2 to 1
- w_gate: bfloat16 [2, 1536, 4096], P(None, 'fsdp'), may hold values from -0.09375 to 0.09375
- w_up: bfloat16 [2, 1536, 4096], P(None, 'fsdp'), may hold values from -0.09375 to 0.09375
- w_down: bfloat16 [2, 1536, 4096], P(None, 'fsdp'), may hold values from -0.15625 to 0.15625
- a_factors: float32 [2, 3, 64, 4096], P(None, None, 'wide', 'fsdp'), may hold values from -0.09375 to 0.09375
- b_factors: float32 [2, 3, 64, 1536], P(None, None, 'wide', 'fsdp'), may hold values from -0.6 to 0.6
Outputs:
- moe_out: bfloat16 [8192, 4096], P('wide', 'fsdp')
The draws below stay inside these ranges and needn't reach their ends.
All inputs are finite; a program needn't handle non-finite values.
Results may differ from the reference program's by a relative error of at most 0.017.
Values may be sent and summed in bfloat16 or wider, within the bound.
A program may use at most 64 MiB of HBM per device.

```python
import math
import jax
import jax.numpy as jnp
from jax import lax

D = 4096
F = 1536
R = 64
EXPERT_COUNT = 2
TOPK = 2
ROWS_ALL = 8192
N_FSDP = 8


def level_of(stream_key, dims, split, low, top_value):
    def one(dim, blocks):
        steps = jax.random.uniform(jax.random.fold_in(jax.random.fold_in(stream_key, 6), dim), (blocks,), jnp.float32, low / len(split), top_value / len(split))
        return jnp.repeat(jnp.exp(steps), dims[dim] // blocks).reshape((-1,) + (1,) * (len(dims) - dim - 1))

    level = one(*split[0])
    for cut in split[1:]:
        level = level * one(*cut)
    return level


def distinct(stream_key, rows, amount, top, lift):
    sequence = jax.random.permutation(jax.random.fold_in(stream_key, 1), amount)
    pull = sequence
    for power in range(3):
        pull = pull * pull // amount
    pull = pull * lift // amount
    tickets = jax.random.randint(jax.random.fold_in(stream_key, 2), (rows, amount), 0, 4096) + pull
    sure = jax.random.permutation(jax.random.fold_in(stream_key, 3), rows)[jnp.arange(amount) % rows]
    tickets = jnp.where(jnp.arange(rows)[:, None] == sure[None, :], 1 << 14, tickets)
    priority = tickets * amount + jnp.arange(amount)
    return lax.top_k(priority.astype(jnp.int32), top)[1].astype(jnp.int32)


def centred(key, shape, spread, most, cuts=(), kind=jnp.bfloat16):
    factor_of = level_of(key, shape, cuts, -0.22, 0.18) if cuts else 1.0
    values = jax.random.normal(key, shape, jnp.float32) * spread * factor_of
    return jnp.minimum(jnp.maximum(values, -most), most).astype(kind)


def setup_inputs(seed: int = 0) -> dict:
    key_of = jax.random.split(jax.random.key(seed), 10)
    return {
        "tokens": centred(key_of[0], (ROWS_ALL, D), 1.0, 6.0, ((0, 32), (1, 8))),
        "norm_gain": jnp.clip(1.0 + 0.18 * jax.random.normal(key_of[1], (D,), jnp.float32), 0.1, 1.9),
        "route_ids": distinct(key_of[2], ROWS_ALL, EXPERT_COUNT, TOPK, 0),
        "route_gates": jnp.clip(jnp.exp(math.log(1.0) - 1.609438 * jax.random.uniform(key_of[3], (ROWS_ALL, TOPK), jnp.float32) ** level_of(key_of[3], (ROWS_ALL, TOPK), ((0, 32),), -0.2, 0.2)), 0.2, 1.0),
        "w_gate": centred(key_of[4], (EXPERT_COUNT, F, D), D ** -0.5, 0.09375, ((1, 8),)),
        "w_up": centred(key_of[5], (EXPERT_COUNT, F, D), D ** -0.5, 0.09375, ((1, 8),)),
        "w_down": centred(key_of[6], (EXPERT_COUNT, F, D), F ** -0.5, 0.15625, ((1, 8),)),
        "a_factors": centred(key_of[7], (EXPERT_COUNT, 3, R, D), D ** -0.5, 0.09375, ((2, 32), (3, 8)), jnp.float32),
        "b_factors": centred(key_of[8], (EXPERT_COUNT, 3, R, F), 0.094, 0.6, ((2, 32), (3, 8)), jnp.float32),
    }


adapter_scale = 2.0

def merge_one(weight_matrix, left, right):
    weight_update = lax.dot_general(left, right, (((0,), (0,)), ((), ())), precision=lax.Precision.HIGHEST, preferred_element_type=jnp.float32)
    return (weight_matrix.astype(jnp.float32) + adapter_scale * weight_update).astype(jnp.bfloat16)

def project_rows(normed, merged):
    return lax.dot_general(normed, merged, (((1,), (1,)), ((), ())), preferred_element_type=jnp.float32)

def reference(tokens, norm_gain, route_ids, route_gates, w_gate, w_up, w_down, a_factors, b_factors):
    value_entries = tokens.astype(jnp.float32)
    mean_square = lax.optimization_barrier(jnp.mean(value_entries * value_entries, axis=-1, keepdims=True))
    normed = (value_entries * lax.rsqrt(mean_square + 1e-06) * norm_gain).astype(jnp.bfloat16)
    labels = jnp.arange(EXPERT_COUNT, dtype=jnp.int32)
    match = (route_ids[:, :, None] == labels[None, None, :]).astype(jnp.float32)
    mix = lax.optimization_barrier(jnp.sum(match * route_gates[:, :, None], axis=1))
    hiddens = []
    downs = []
    for expert in range(EXPERT_COUNT):
        merged_gate = merge_one(w_gate[expert], b_factors[expert, 0], a_factors[expert, 0])
        merged_up = merge_one(w_up[expert], b_factors[expert, 1], a_factors[expert, 1])
        merged_down = merge_one(w_down[expert], b_factors[expert, 2], a_factors[expert, 2])
        gate_act = project_rows(normed, merged_gate)
        up_act = project_rows(normed, merged_up)
        hiddens.append((jax.nn.silu(gate_act) * up_act * mix[:, expert:expert + 1]).astype(jnp.bfloat16))
        downs.append(merged_down)
    block = F // N_FSDP
    total = jnp.zeros((tokens.shape[0], tokens.shape[1]), jnp.float32)
    for shard in range(N_FSDP):
        partial_value = jnp.zeros((tokens.shape[0], tokens.shape[1]), jnp.float32)
        for expert in range(EXPERT_COUNT):
            hidden_block = hiddens[expert][:, shard * block:(shard + 1) * block]
            down_proj_block = downs[expert][shard * block:(shard + 1) * block]
            partial_value = partial_value + jnp.dot(hidden_block, down_proj_block, preferred_element_type=jnp.float32)
        total = total + partial_value.astype(jnp.bfloat16).astype(jnp.float32)
    return total.astype(jnp.bfloat16)
```

```python
import functools

import jax
import jax.numpy as jnp
from jax import lax
from jax.experimental import pallas as pl
from jax.experimental.pallas import tpu as pltpu
from jax.sharding import PartitionSpec as P

F32, BF16 = jnp.float32, jnp.bfloat16
MESH = pl.DeviceIdType.MESH
ROWS, COLS, HID, WIDTH = 256, 512, 192, 4096
HALF, QUART = 128, 64
UB = 32


def dot_nt(a, b):
    return lax.dot_general(a, b, (((1,), (1,)), ((), ())), preferred_element_type=F32)


def dot_nn(a, b):
    return jnp.dot(a, b, preferred_element_type=F32)


def iota(shape, dim):
    return lax.broadcasted_iota(jnp.int32, shape, dim)


def body(
    x_ref, gain_ref, ids_ref, gates_ref, wg_hbm, wu_hbm, wd_hbm, a_ref, b_ref, out_ref,
    w_in, w_down, packet, fac, top, bot, b_exp, bd_t, ad_c,
    xb, acc, sq, hid,
    u_part, u_in, u_blk, u_all, v_part, v_in, v_blk, v_all,
    s1, s2p, s2m, s3, s4p, s4m, s5, r1, r2p, r2m, r3, r4p, r4m, r5,
    wsem, ssem, rsem,
):
    w = lax.axis_index("wide")
    f = lax.axis_index("fsdp")
    zh, xx, core = w // 8, (w // 2) % 4, w % 2
    y, z = f // 2, f % 2

    def fs(dy, flip):
        zz = 1 - z if flip else z
        return ((y + dy) % 4) * 2 + zz

    def wide_at(dzh, dx, dcore):
        return (((zh + dzh) % 4) * 4 + (xx + dx) % 4) * 2 + (core + dcore) % 2

    up, down, across = (w, fs(1, False)), (w, fs(3, False)), (w, fs(0, True))
    count = [0]

    def remote(src, dst, dev):
        i = count[0]
        count[0] += 1
        return pltpu.make_async_remote_copy(
            src_ref=src, dst_ref=dst, send_sem=ssem.at[i], recv_sem=rsem.at[i],
            device_id=dev, device_id_type=MESH,
        )

    loads = []
    for e in range(2):
        for j, (ref, dst) in enumerate(((wg_hbm, w_in.at[pl.ds(e * HID, HID)]),
                                        (wu_hbm, w_in.at[pl.ds((2 + e) * HID, HID)]),
                                        (wd_hbm, w_down.at[pl.ds(e * HID, HID)]))):
            c = pltpu.make_async_copy(ref.at[e], dst, wsem.at[e * 3 + j])
            c.start()
            loads.append(c)

    peers = [(wide_at(d, 0, 0), f) for d in (1, 2, 3)] + [(wide_at(0, d, 0), f) for d in (1, 2, 3)]
    peers += [(wide_at(0, 0, 1), f)] + [(w, (f + i) % 8) for i in range(1, 8)]
    barrier = pltpu.get_barrier_semaphore()
    for p in peers:
        pl.semaphore_signal(barrier, inc=1, device_id=p, device_id_type=MESH)

    packet[...] = jnp.zeros_like(packet)
    for e in range(2):
        for p in range(2):
            r = e * 4 + p * 2
            packet[r:r + 2, 0:512] = a_ref[e, p]
            packet[r:r + 2, 512:704] = b_ref[e, p]
        for h in range(2):
            packet[h * 4 + e * 2:h * 4 + e * 2 + 2, 768:1024] = a_ref[e, 2, :, h * 256:(h + 1) * 256]
        packet[e * 2:e * 2 + 2, 1024:1216] = b_ref[e, 2]
    fac[0, 0, 0] = jnp.concatenate([packet[:, 0:640], packet[:, 640:1280]], axis=0).astype(BF16)

    pl.semaphore_wait(barrier, len(peers))

    def half(ref, h):
        return ref.at[pl.ds(h * HALF, HALF)]

    def quart(ref, h, q):
        return ref.at[pl.ds(h * HALF + q * QUART, QUART)]

    fz = [remote(fac.at[0, 0, 0], fac.at[0, 0, 4 - d], (wide_at(d, 0, 0), f)) for d in (1, 2, 3)]
    fx = [remote(fac.at[0, 0], fac.at[0, 4 - d], (wide_at(0, d, 0), f)) for d in (1, 2, 3)]
    fc = [remote(fac.at[0, d], fac.at[1, d], (wide_at(0, 0, 1), f)) for d in range(4)]
    tok = []
    for h in range(2):
        t = {}
        t["up"] = remote(half(x_ref, h), half(xb.at[0], h), up)
        t["down"] = remote(half(x_ref, h), half(xb.at[1], h), down)
        t["across"] = remote(half(x_ref, h), half(xb.at[2], h), across)
        t["far0"] = remote(quart(xb.at[0], h, 0), quart(xb.at[3], h, 0), up)
        t["far1"] = remote(quart(xb.at[1], h, 1), quart(xb.at[3], h, 1), down)
        t["dup"] = remote(half(xb.at[2], h), half(xb.at[4], h), up)
        t["ddown"] = remote(half(xb.at[2], h), half(xb.at[5], h), down)
        t["dfar"] = remote(half(xb.at[3], h), half(xb.at[6], h), across)
        tok.append(t)
    src = [fs(3, False), fs(1, False), fs(0, True), fs(2, False), fs(3, True), fs(1, True), fs(2, True)]
    other = [(w, (f + i) % 8) for i in range(1, 8)]
    mine = pl.ds(pl.multiple_of(f * UB, UB), UB)

    def rows_of(i):
        return pl.ds(pl.multiple_of(((f + i) % 8) * UB, UB), UB)

    u_rs = [remote(u_part.at[rows_of(i)], u_in.at[i - 1], other[i - 1]) for i in range(1, 8)]
    u_ag = [remote(u_blk, u_all.at[mine], other[i - 1]) for i in range(1, 8)]
    v_rs = [remote(v_part.at[rows_of(i)], v_in.at[i - 1], other[i - 1]) for i in range(1, 8)]
    v_ag = [remote(v_blk, v_all.at[mine], other[i - 1]) for i in range(1, 8)]
    red = []
    for h in range(2):
        t = {}
        t["t1"] = remote(half(s1, h), half(r1, h), across)
        t["t2p"] = remote(half(s2p, h), half(r2m, h), up)
        t["t2m"] = remote(half(s2m, h), half(r2p, h), down)
        t["t3p"] = remote(quart(s3, h, 0), quart(r3, h, 0), up)
        t["t3m"] = remote(quart(s3, h, 1), quart(r3, h, 1), down)
        t["t4p0"] = remote(quart(s4p, h, 0), quart(r4m, h, 0), up)
        t["t4p1"] = remote(quart(s4p, h, 1), quart(r4m, h, 1), up)
        t["t4m0"] = remote(quart(s4m, h, 0), quart(r4p, h, 0), down)
        t["t4m1"] = remote(quart(s4m, h, 1), quart(r4p, h, 1), down)
        t["t5"] = remote(half(s5, h), half(r5, h), across)
        red.append(t)

    def start(h, *names):
        for n in names:
            tok[h][n].start()

    def got(h, *names):
        for n in names:
            tok[h][n].wait_recv()

    def rstart(h, *names):
        for n in names:
            red[h][n].start()

    def rgot(h, *names):
        for n in names:
            red[h][n].wait_recv()

    def scaled(ref, h, owner):
        lanes = pl.ds(pl.multiple_of(owner * COLS, COLS), COLS)
        v = ref[pl.ds(h * HALF, HALF), :].astype(F32)
        s = v * v
        s = (s[:, 0:128] + s[:, 128:256]) + (s[:, 256:384] + s[:, 384:512])
        return (v * gain_ref[:, lanes]).astype(BF16), s, lanes

    def project(ref, h, owner, first=False):
        xg, s, lanes = scaled(ref, h, owner)
        rows = pl.ds(h * HALF, HALF)
        prod = dot_nt(xg, w_in[:, lanes])
        if first:
            acc[rows, :] = prod
            sq[rows, :] = s
        else:
            acc[rows, :] += prod
            sq[rows, :] += s

    def block(h, owner):
        lanes = pl.ds(pl.multiple_of(owner * COLS, COLS), COLS)
        return dot_nn(hid[pl.ds(h * HALF, HALF), :], w_down[:, lanes])

    def activate(h):
        rows = pl.ds(h * HALF, HALF)
        mean = jnp.sum(sq[rows, :], axis=-1, keepdims=True) * (1.0 / WIDTH)
        scale = lax.rsqrt(mean + 1e-06)
        pre = (acc[rows, :] + dot_nn(u_all[rows, :], b_exp[...])) * scale
        g, u = pre[:, 0:2 * HID], pre[:, 2 * HID:4 * HID]
        ids, gates = ids_ref[rows, :], gates_ref[rows, :]
        mix = [jnp.sum(jnp.where(ids == e, gates, 0.0), axis=-1, keepdims=True) for e in range(2)]
        m = jnp.where(iota((HALF, 2 * HID), 1) < HID, mix[0], mix[1])
        hid[rows, :] = (g / (1.0 + jnp.exp(-g)) * u * m).astype(BF16)

    def send_free(h):
        rows = pl.ds(h * HALF, HALF)
        s1[rows, :] = block(h, fs(2, True)).astype(BF16)
        rstart(h, "t1")
        s2p[rows, :] = block(h, fs(1, True)).astype(BF16)
        rstart(h, "t2p")
        s2m[rows, :] = block(h, fs(3, True)).astype(BF16)
        rstart(h, "t2m")
        s4p[rows, :] = block(h, fs(1, False)).astype(BF16)
        rstart(h, "t4p1")
        s4m[rows, :] = block(h, fs(3, False)).astype(BF16)
        rstart(h, "t4m0")

    def send_far(h):
        rows = pl.ds(h * HALF, HALF)
        part = block(h, fs(2, False))
        rgot(h, "t1")
        s3[rows, :] = (part + r1[rows, :].astype(F32)).astype(BF16)
        rstart(h, "t3p", "t3m")

    def send_across(h):
        rows = pl.ds(h * HALF, HALF)
        part = block(h, fs(0, True))
        rgot(h, "t2p", "t2m")
        s5[rows, :] = (part + r2p[rows, :].astype(F32) + r2m[rows, :].astype(F32)).astype(BF16)
        rstart(h, "t5")

    def send_near(h):
        q0, q1 = pl.ds(h * HALF, QUART), pl.ds(h * HALF + QUART, QUART)
        rgot(h, "t3p")
        s4p[q0, :] = (s4p[q0, :].astype(F32) + r3[q0, :].astype(F32)).astype(BF16)
        rstart(h, "t4p0")
        rgot(h, "t3m")
        s4m[q1, :] = (s4m[q1, :].astype(F32) + r3[q1, :].astype(F32)).astype(BF16)
        rstart(h, "t4m1")

    def finish(h):
        rows = pl.ds(h * HALF, HALF)
        part = block(h, f) + dot_nn(v_all[rows, :], ad_c[...])
        rgot(h, "t4p0", "t4p1", "t4m0", "t4m1", "t5")
        part = part + r4p[rows, :].astype(F32) + r4m[rows, :].astype(F32) + r5[rows, :].astype(F32)
        out_ref[rows, :] = part.astype(BF16)

    def exchange_sum(part, arrived, blk, whole, rs, ag):
        total = part[mine, :].astype(F32)
        for i in range(7):
            rs[i].wait_recv()
            total = total + arrived[i].astype(F32)
        blk[...] = total.astype(BF16)
        whole[mine, :] = total.astype(BF16)
        for c in ag:
            c.start()

    for c in fz:
        c.start()
    start(0, "across", "up", "down")
    start(1, "across", "up", "down")
    for c in fz:
        c.wait_recv()
    for c in fx:
        c.start()
    fc[0].start()
    got(0, "across", "up", "down")
    start(0, "far0", "far1", "dup", "ddown")
    for c in loads:
        c.wait()
    project(x_ref, 0, f, True)
    for d in (1, 2, 3):
        fx[3 - d].wait_recv()
        fc[d].start()
    project(x_ref, 1, f, True)
    project(xb.at[2], 0, src[2])
    got(1, "across", "up", "down")
    start(1, "far0", "far1", "dup", "ddown")
    got(0, "far0", "far1")
    start(0, "dfar")
    for c in fc:
        c.wait_recv()

    def unpack(i, carry):
        rows = pl.ds(pl.multiple_of(i * 16, 16), 16)
        two = [fac[i // 8, (i // 2) % 4, (i % 2) * 2 + k].astype(F32) for k in range(2)]
        top[rows, :] = jnp.concatenate([two[0][0:8], two[1][0:8]], axis=0).astype(BF16)
        bot[rows, :] = jnp.concatenate([two[0][8:16], two[1][8:16]], axis=0).astype(BF16)
        return carry

    lax.fori_loop(0, 16, unpack, 0)
    for h in range(2):
        xg, _, _ = scaled(x_ref, h, f)
        u_part[pl.ds(h * HALF, HALF), :] = dot_nt(xg, top[:, 0:512]).astype(BF16)
    for c in u_rs:
        c.start()
    project(xb.at[0], 0, src[0])
    project(xb.at[1], 0, src[1])
    rep = (iota((256, 4 * HID), 0) == iota((256, 4 * HID), 1) % HID).astype(BF16)
    b_in = jnp.concatenate([top[:, 512:640], bot[:, 0:128]], axis=1)
    k, j = iota((256, 4 * HID), 0), iota((256, 4 * HID), 1) // HID
    keep = ((k % 8) // 4 + 2 * ((k % 4) // 2)) == j
    b_exp[...] = jnp.where(keep, 2.0 * dot_nn(b_in, rep), 0.0).astype(BF16)
    got(1, "far0", "far1")
    start(1, "dfar")
    exchange_sum(u_part, u_in, u_blk, u_all, u_rs, u_ag)
    r, k = iota((128, 256), 0), iota((128, 256), 1)
    slot = (r // 4) * 8 + r % 4
    sel0, sel1 = (k == slot).astype(BF16), (k == slot + 4).astype(BF16)
    bd = dot_nn(sel0, bot[:, 384:640]).astype(BF16)
    r, j = iota((128, 2 * HID), 0), iota((128, 2 * HID), 1) // HID
    bd_t[...] = jnp.where((r % 4) // 2 == j, dot_nn(bd, rep[:, 0:2 * HID]), 0.0).astype(BF16)
    ad_c[:, 0:256] = (2.0 * dot_nn(sel0, bot[:, 128:384])).astype(BF16)
    ad_c[:, 256:512] = (2.0 * dot_nn(sel1, bot[:, 128:384])).astype(BF16)
    project(xb.at[3], 0, src[3])
    for i in range(4):
        project(xb.at[i], 1, src[i])
    got(0, "dup", "ddown")
    project(xb.at[4], 0, src[4])
    project(xb.at[5], 0, src[5])
    got(0, "dfar")
    project(xb.at[6], 0, src[6])
    for c in u_ag:
        c.wait_recv()
    activate(0)
    send_free(0)
    got(1, "dup", "ddown")
    project(xb.at[4], 1, src[4])
    project(xb.at[5], 1, src[5])
    got(1, "dfar")
    project(xb.at[6], 1, src[6])
    activate(1)
    v_part[...] = dot_nt(hid[...], bd_t[...]).astype(BF16)
    for c in v_rs:
        c.start()
    send_far(0)
    send_free(1)
    send_across(0)
    exchange_sum(v_part, v_in, v_blk, v_all, v_rs, v_ag)
    send_far(1)
    send_near(0)
    send_across(1)
    for c in v_ag:
        c.wait_recv()
    finish(0)
    send_near(1)
    finish(1)
    for c in fz + fx + fc + u_rs + u_ag + v_rs + v_ag:
        c.wait_send()
    for t in tok + red:
        for c in t.values():
            c.wait_send()


N_COPIES = 3 + 3 + 4 + 16 + 28 + 20


def per_device(tokens, norm_gain, route_ids, route_gates, w_gate, w_up, w_down, a_factors, b_factors):
    vmem = pl.BlockSpec(memory_space=pltpu.VMEM)
    hbm = pl.BlockSpec(memory_space=pl.ANY)
    block = pltpu.VMEM((ROWS, COLS), BF16)
    return pl.pallas_call(
        body,
        out_shape=jax.ShapeDtypeStruct((ROWS, COLS), BF16),
        in_specs=[vmem, vmem, vmem, vmem, hbm, hbm, hbm, vmem, vmem],
        out_specs=vmem,
        scratch_shapes=[
            pltpu.VMEM((4 * HID, WIDTH), BF16),
            pltpu.VMEM((2 * HID, WIDTH), BF16),
            pltpu.VMEM((8, 1280), F32),
            pltpu.VMEM((2, 4, 4, 16, 640), BF16),
            pltpu.VMEM((256, 640), BF16),
            pltpu.VMEM((256, 640), BF16),
            pltpu.VMEM((256, 4 * HID), BF16),
            pltpu.VMEM((128, 2 * HID), BF16),
            pltpu.VMEM((128, COLS), BF16),
            pltpu.VMEM((7, ROWS, COLS), BF16),
            pltpu.VMEM((ROWS, 4 * HID), F32),
            pltpu.VMEM((ROWS, 128), F32),
            pltpu.VMEM((ROWS, 2 * HID), BF16),
            pltpu.VMEM((ROWS, 256), BF16),
            pltpu.VMEM((7, UB, 256), BF16),
            pltpu.VMEM((UB, 256), BF16),
            pltpu.VMEM((ROWS, 256), BF16),
            pltpu.VMEM((ROWS, 128), BF16),
            pltpu.VMEM((7, UB, 128), BF16),
            pltpu.VMEM((UB, 128), BF16),
            pltpu.VMEM((ROWS, 128), BF16),
        ] + [block] * 14 + [
            pltpu.SemaphoreType.DMA((6,)),
            pltpu.SemaphoreType.DMA((N_COPIES,)),
            pltpu.SemaphoreType.DMA((N_COPIES,)),
        ],
        compiler_params=pltpu.CompilerParams(
            collective_id=0, has_side_effects=True, vmem_limit_bytes=48 * 2**20
        ),
    )(tokens, norm_gain.reshape(1, WIDTH), route_ids, route_gates, w_gate, w_up, w_down, a_factors, b_factors)


def solution(mesh):
    placed = (
        P("wide", "fsdp"),
        P(),
        P("wide", None),
        P("wide", None),
        P(None, "fsdp", None),
        P(None, "fsdp", None),
        P(None, "fsdp", None),
        P(None, None, "wide", "fsdp"),
        P(None, None, "wide", "fsdp"),
    )
    return jax.shard_map(
        per_device, mesh=mesh, in_specs=placed, out_specs=P("wide", "fsdp"), check_vma=False
    )
```

```python
import functools

import jax
import jax.numpy as jnp
from jax import lax
from jax.experimental import pallas as pl
from jax.experimental.pallas import tpu as pltpu
from jax.sharding import PartitionSpec as P

F32, BF16 = jnp.float32, jnp.bfloat16
MESH = pl.DeviceIdType.MESH
ROWS, COLS, HID, WIDTH = 256, 512, 192, 4096
HALF, QUART = 128, 64
UB = 32


def dot_nt(a, b):
    return lax.dot_general(a, b, (((1,), (1,)), ((), ())), preferred_element_type=F32)


def dot_nn(a, b):
    return jnp.dot(a, b, preferred_element_type=F32)


def iota(shape, dim):
    return lax.broadcasted_iota(jnp.int32, shape, dim)


def body(
    x_hbm, gain_hbm, ids_hbm, gates_hbm, wg_hbm, wu_hbm, wd_hbm, a_hbm, b_hbm, out_ref,
    x_ref, gain_ref, ids_ref, gates_ref, a_ref, b_ref, w_in, w_down, pack_a, pack_b, fac_a, fac_b, fa, fb, b_exp, bd_t, ad_c, mixed,
    xb, acc, sq, hid,
    u_part, u_in, u_blk, u_all, v_part, v_in, v_blk, v_all,
    s1, s2p, s2m, s3, s4p, s4m, s5, r1, r2p, r2m, r3, r4p, r4m, r5,
    wsem, ssem, rsem,
):
    w = lax.axis_index("wide")
    f = lax.axis_index("fsdp")
    zh, xx, core = w // 8, (w // 2) % 4, w % 2
    y, z = f // 2, f % 2

    def fs(dy, flip):
        zz = 1 - z if flip else z
        return ((y + dy) % 4) * 2 + zz

    def wide_at(dzh, dx, dcore):
        return (((zh + dzh) % 4) * 4 + (xx + dx) % 4) * 2 + (core + dcore) % 2

    up, down, across = (w, fs(1, False)), (w, fs(3, False)), (w, fs(0, True))
    count = [0]

    def remote(src, dst, dev):
        i = count[0]
        count[0] += 1
        return pltpu.make_async_remote_copy(
            src_ref=src, dst_ref=dst, send_sem=ssem.at[i], recv_sem=rsem.at[i],
            device_id=dev, device_id_type=MESH,
        )

    small = [
        pltpu.make_async_copy(src, dst, wsem.at[6 + i])
        for i, (src, dst) in enumerate((
            (a_hbm, a_ref), (b_hbm, b_ref), (x_hbm, x_ref),
            (gain_hbm, gain_ref), (ids_hbm, ids_ref), (gates_hbm, gates_ref),
        ))
    ]
    for c in small:
        c.start()
    loads = []
    for e in range(2):
        for j, (ref, dst) in enumerate(((wg_hbm, w_in.at[pl.ds(e * HID, HID)]),
                                        (wu_hbm, w_in.at[pl.ds((2 + e) * HID, HID)]),
                                        (wd_hbm, w_down.at[pl.ds(e * HID, HID)]))):
            c = pltpu.make_async_copy(ref.at[e], dst, wsem.at[e * 3 + j])
            c.start()
            loads.append(c)

    peers = [(wide_at(d // 2, 0, d % 2), f) for d in range(1, 8)] + [(wide_at(0, d, 0), f) for d in (1, 2, 3)]
    peers += [(w, (f + i) % 8) for i in range(1, 8)]
    barrier = pltpu.get_barrier_semaphore()
    for p in peers:
        pl.semaphore_signal(barrier, inc=1, device_id=p, device_id_type=MESH)

    small[0].wait()
    for e in range(2):
        for p in range(2):
            pack_a[e * 4 + p * 2:e * 4 + p * 2 + 2, :] = a_ref[e, p]
    fac_a[0, 0, 0] = jnp.concatenate([pack_a[:, 0:256], pack_a[:, 256:512]], axis=0).astype(BF16)

    def pack_second():
        pack_b[...] = jnp.zeros_like(pack_b)
        for e in range(2):
            for p in range(2):
                pack_b[e * 4 + p * 2:e * 4 + p * 2 + 2, 0:192] = b_ref[e, p]
            for h in range(2):
                pack_b[h * 4 + e * 2:h * 4 + e * 2 + 2, 256:512] = a_ref[e, 2, :, h * 256:(h + 1) * 256]
            pack_b[e * 2:e * 2 + 2, 512:704] = b_ref[e, 2]
        fac_b[0, 0, 0] = jnp.concatenate([pack_b[:, 0:384], pack_b[:, 384:768]], axis=0).astype(BF16)

    for c in small[1:]:
        c.wait()
    pl.semaphore_wait(barrier, len(peers))

    def half(ref, h):
        return ref.at[pl.ds(h * HALF, HALF)]

    def quart(ref, h, q):
        return ref.at[pl.ds(h * HALF + q * QUART, QUART)]

    near = [(dz, dc) for dc in (0, 1) for dz in (2, 1, 3, 0) if dz or dc]

    def factor_copies(fac):
        by_z = [
            remote(fac.at[0, 0, 0], fac.at[0, dc, (4 - dz) % 4], (wide_at(dz, 0, dc), f)) for dz, dc in near
        ]
        by_x = [remote(fac.at[0], fac.at[4 - d], (wide_at(0, d, 0), f)) for d in (2, 1, 3)]
        return by_z, by_x

    az, ax = factor_copies(fac_a)
    bz, bx = factor_copies(fac_b)
    tok = []
    for h in range(2):
        t = {}
        t["up"] = remote(half(x_ref, h), half(xb.at[0], h), up)
        t["down"] = remote(half(x_ref, h), half(xb.at[1], h), down)
        t["across"] = remote(half(x_ref, h), half(xb.at[2], h), across)
        t["far0"] = remote(quart(xb.at[0], h, 0), quart(xb.at[3], h, 0), up)
        t["far1"] = remote(quart(xb.at[1], h, 1), quart(xb.at[3], h, 1), down)
        t["dup"] = remote(half(xb.at[2], h), half(xb.at[4], h), up)
        t["ddown"] = remote(half(xb.at[2], h), half(xb.at[5], h), down)
        t["dfar"] = remote(half(xb.at[3], h), half(xb.at[6], h), across)
        tok.append(t)
    src = [fs(3, False), fs(1, False), fs(0, True), fs(2, False), fs(3, True), fs(1, True), fs(2, True)]
    other = [(w, (f + i) % 8) for i in range(1, 8)]
    mine = pl.ds(pl.multiple_of(f * UB, UB), UB)

    def rows_of(i):
        return pl.ds(pl.multiple_of(((f + i) % 8) * UB, UB), UB)

    u_rs = [remote(u_part.at[rows_of(i)], u_in.at[i - 1], other[i - 1]) for i in range(1, 8)]
    u_ag = [remote(u_blk, u_all.at[mine], other[i - 1]) for i in range(1, 8)]
    v_rs = [remote(v_part.at[rows_of(i)], v_in.at[i - 1], other[i - 1]) for i in range(1, 8)]
    v_ag = [remote(v_blk, v_all.at[mine], other[i - 1]) for i in range(1, 8)]
    red = []
    for h in range(2):
        t = {}
        t["t1"] = remote(half(s1, h), half(r1, h), across)
        t["t2p"] = remote(half(s2p, h), half(r2m, h), up)
        t["t2m"] = remote(half(s2m, h), half(r2p, h), down)
        t["t3p"] = remote(quart(s3, h, 0), quart(r3, h, 0), up)
        t["t3m"] = remote(quart(s3, h, 1), quart(r3, h, 1), down)
        t["t4p0"] = remote(quart(s4p, h, 0), quart(r4m, h, 0), up)
        t["t4p1"] = remote(quart(s4p, h, 1), quart(r4m, h, 1), up)
        t["t4m0"] = remote(quart(s4m, h, 0), quart(r4p, h, 0), down)
        t["t4m1"] = remote(quart(s4m, h, 1), quart(r4p, h, 1), down)
        t["t5"] = remote(half(s5, h), half(r5, h), across)
        red.append(t)

    def start(h, *names):
        for n in names:
            tok[h][n].start()

    def got(h, *names):
        for n in names:
            tok[h][n].wait_recv()

    def rstart(h, *names):
        for n in names:
            red[h][n].start()

    def rgot(h, *names):
        for n in names:
            red[h][n].wait_recv()

    def scaled(ref, owner):
        lanes = pl.ds(pl.multiple_of(owner * COLS, COLS), COLS)
        v = ref[...].astype(F32)
        s = v * v
        s = (s[:, 0:128] + s[:, 128:256]) + (s[:, 256:384] + s[:, 384:512])
        return (v * gain_ref[:, lanes]).astype(BF16), s, lanes

    def project(ref, owner, first=False):
        xg, s, lanes = scaled(ref, owner)
        prod = dot_nt(xg, w_in[:, lanes])
        if first:
            acc[...] = prod
            sq[...] = s
        else:
            acc[...] += prod
            sq[...] += s

    def block(owner):
        lanes = pl.ds(pl.multiple_of(owner * COLS, COLS), COLS)
        return dot_nn(hid[...], w_down[:, lanes])

    def activate():
        mean = jnp.sum(sq[...], axis=-1, keepdims=True) * (1.0 / WIDTH)
        scale = lax.rsqrt(mean + 1e-06)
        pre = (acc[...] + dot_nn(u_all[...], b_exp[...])) * scale
        g, u = pre[:, 0:2 * HID], pre[:, 2 * HID:4 * HID]
        hid[...] = (g / (1.0 + jnp.exp(-g)) * u * mixed[...]).astype(BF16)

    def mix_rows():
        ids, gates = ids_ref[...], gates_ref[...]
        mix = [jnp.sum(jnp.where(ids == e, gates, 0.0), axis=0, keepdims=True) for e in range(2)]
        r = iota((8, ROWS), 0)
        mix = jnp.where(r == 0, mix[0], jnp.where(r == 1, mix[1], 0.0))
        pick = (iota((8, 2 * HID), 0) == iota((8, 2 * HID), 1) // HID).astype(F32)
        mixed[...] = lax.dot_general(
            mix, pick, (((0,), (0,)), ((), ())), precision=lax.Precision.HIGHEST, preferred_element_type=F32
        )

    def to_block(dst, owner):
        dst[...] = block(owner).astype(BF16)

    def rows_half(h):
        return pl.ds(h * HALF, HALF)

    def send_far(h):
        rows = rows_half(h)
        rgot(h, "t1")
        s3[rows, :] = (s3[rows, :].astype(F32) + r1[rows, :].astype(F32)).astype(BF16)
        rstart(h, "t3p", "t3m")

    def send_across(h):
        rows = rows_half(h)
        rgot(h, "t2p", "t2m")
        s5[rows, :] = (
            s5[rows, :].astype(F32) + r2p[rows, :].astype(F32) + r2m[rows, :].astype(F32)
        ).astype(BF16)
        rstart(h, "t5")

    def send_near(h):
        q0, q1 = pl.ds(h * HALF, QUART), pl.ds(h * HALF + QUART, QUART)
        rgot(h, "t3p")
        s4p[q0, :] = (s4p[q0, :].astype(F32) + r3[q0, :].astype(F32)).astype(BF16)
        rstart(h, "t4p0")
        rgot(h, "t3m")
        s4m[q1, :] = (s4m[q1, :].astype(F32) + r3[q1, :].astype(F32)).astype(BF16)
        rstart(h, "t4m1")

    def finish(h):
        rows = rows_half(h)
        rgot(h, "t5", "t4p1", "t4m0", "t4p0", "t4m1")
        part = acc[rows, 0:COLS] + r4p[rows, :].astype(F32) + r4m[rows, :].astype(F32) + r5[rows, :].astype(F32)
        out_ref[rows, :] = part.astype(BF16)

    def exchange_sum(part, arrived, blk, whole, rs, ag):
        total = part[mine, :].astype(F32)
        for i in range(7):
            rs[i].wait_recv()
            total = total + arrived[i].astype(F32)
        blk[...] = total.astype(BF16)
        whole[mine, :] = total.astype(BF16)
        for c in ag:
            c.start()

    def over_x(by_z, by_x):
        for c in by_z:
            c.wait_recv()
        for c in by_x:
            c.start()

    def unpack(fac, whole, width):
        def step(i, carry):
            rows = pl.ds(pl.multiple_of(i * 16, 16), 16)
            two = [fac[i // 4, (i // 2) % 2, (i % 2) * 2 + k].astype(F32) for k in range(2)]
            whole[rows, 0:width] = jnp.concatenate([two[0][0:8], two[1][0:8]], axis=0).astype(BF16)
            whole[rows, width:2 * width] = jnp.concatenate([two[0][8:16], two[1][8:16]], axis=0).astype(BF16)
            return carry

        lax.fori_loop(0, 16, step, 0)

    def prepare():
        rep = (iota((256, 4 * HID), 0) == iota((256, 4 * HID), 1) % HID).astype(BF16)
        k, j = iota((256, 4 * HID), 0), iota((256, 4 * HID), 1) // HID
        keep = ((k % 8) // 4 + 2 * ((k % 4) // 2)) == j
        b_exp[...] = jnp.where(keep, 2.0 * dot_nn(fb[:, 0:256], rep), 0.0).astype(BF16)
        r, k = iota((128, 256), 0), iota((128, 256), 1)
        slot = (r // 4) * 8 + r % 4
        sel0, sel1 = (k == slot).astype(BF16), (k == slot + 4).astype(BF16)
        bd = dot_nn(sel0, fb[:, 512:768]).astype(BF16)
        r, j = iota((128, 2 * HID), 0), iota((128, 2 * HID), 1) // HID
        bd_t[...] = jnp.where((r % 4) // 2 == j, dot_nn(bd, rep[:, 0:2 * HID]), 0.0).astype(BF16)
        ad_c[:, 0:256] = (2.0 * dot_nn(sel0, fb[:, 256:512])).astype(BF16)
        ad_c[:, 256:512] = (2.0 * dot_nn(sel1, fb[:, 256:512])).astype(BF16)

    for c in az:
        c.start()
    start(0, "up", "down", "across")
    start(1, "up", "down", "across")
    pack_second()
    for c in bz:
        c.start()
    for c in loads:
        c.wait()
    project(x_ref, f, True)
    mix_rows()
    over_x(az, ax)
    got(0, "up")
    start(0, "far0")
    got(0, "down")
    start(0, "far1")
    got(1, "up")
    start(1, "far0")
    got(1, "down")
    start(1, "far1")
    project(xb.at[0], src[0])
    got(0, "across")
    start(0, "dup", "ddown")
    for c in ax:
        c.wait_recv()
    unpack(fac_a, fa, 256)
    xg, _, _ = scaled(x_ref, f)
    u_part[...] = dot_nt(xg, fa[...]).astype(BF16)
    for c in u_rs:
        c.start()
    got(1, "across")
    start(1, "dup", "ddown")
    got(0, "far0", "far1")
    start(0, "dfar")
    over_x(bz, bx)
    got(1, "far0", "far1")
    start(1, "dfar")
    project(xb.at[1], src[1])
    project(xb.at[2], src[2])
    exchange_sum(u_part, u_in, u_blk, u_all, u_rs, u_ag)
    project(xb.at[3], src[3])
    for c in bx:
        c.wait_recv()
    unpack(fac_b, fb, 384)
    prepare()
    got(0, "dup", "ddown")
    got(1, "dup", "ddown")
    project(xb.at[4], src[4])
    project(xb.at[5], src[5])
    got(0, "dfar")
    got(1, "dfar")
    project(xb.at[6], src[6])
    for c in u_ag:
        c.wait_recv()
    activate()
    to_block(s1, fs(2, True))
    rstart(0, "t1")
    rstart(1, "t1")
    to_block(s2p, fs(1, True))
    rstart(0, "t2p")
    to_block(s2m, fs(3, True))
    rstart(0, "t2m")
    to_block(s4p, fs(1, False))
    rstart(0, "t4p1")
    to_block(s4m, fs(3, False))
    rstart(0, "t4m0")
    rstart(1, "t2p", "t2m")
    v_part[...] = dot_nt(hid[...], bd_t[...]).astype(BF16)
    for c in v_rs:
        c.start()
    to_block(s3, fs(2, False))
    send_far(0)
    to_block(s5, fs(0, True))
    acc[:, 0:COLS] = block(f)
    send_far(1)
    rstart(1, "t4p1", "t4m0")
    send_across(0)
    send_near(0)
    exchange_sum(v_part, v_in, v_blk, v_all, v_rs, v_ag)
    send_across(1)
    send_near(1)
    for c in v_ag:
        c.wait_recv()
    acc[:, 0:COLS] += dot_nn(v_all[...], ad_c[...])
    finish(0)
    finish(1)
    for c in az + ax + bz + bx + u_rs + u_ag + v_rs + v_ag:
        c.wait_send()
    for t in tok + red:
        for c in t.values():
            c.wait_send()


N_COPIES = 20 + 16 + 28 + 20


def per_device(tokens, norm_gain, route_ids, route_gates, w_gate, w_up, w_down, a_factors, b_factors):
    vmem = pl.BlockSpec(memory_space=pltpu.VMEM)
    hbm = pl.BlockSpec(memory_space=pl.ANY)
    block = pltpu.VMEM((ROWS, COLS), BF16)
    return pl.pallas_call(
        body,
        out_shape=jax.ShapeDtypeStruct((ROWS, COLS), BF16),
        in_specs=[hbm] * 9,
        out_specs=vmem,
        scratch_shapes=[
            pltpu.VMEM((ROWS, COLS), BF16),
            pltpu.VMEM((1, WIDTH), F32),
            pltpu.VMEM((2, ROWS), jnp.int32),
            pltpu.VMEM((2, ROWS), F32),
            pltpu.VMEM((2, 3, 2, COLS), F32),
            pltpu.VMEM((2, 3, 2, HID), F32),
            pltpu.VMEM((4 * HID, WIDTH), BF16),
            pltpu.VMEM((2 * HID, WIDTH), BF16),
            pltpu.VMEM((8, 512), F32),
            pltpu.VMEM((8, 768), F32),
            pltpu.VMEM((4, 2, 4, 16, 256), BF16),
            pltpu.VMEM((4, 2, 4, 16, 384), BF16),
            pltpu.VMEM((256, 512), BF16),
            pltpu.VMEM((256, 768), BF16),
            pltpu.VMEM((256, 4 * HID), BF16),
            pltpu.VMEM((128, 2 * HID), BF16),
            pltpu.VMEM((128, COLS), BF16),
            pltpu.VMEM((ROWS, 2 * HID), F32),
            pltpu.VMEM((7, ROWS, COLS), BF16),
            pltpu.VMEM((ROWS, 4 * HID), F32),
            pltpu.VMEM((ROWS, 128), F32),
            pltpu.VMEM((ROWS, 2 * HID), BF16),
            pltpu.VMEM((ROWS, 256), BF16),
            pltpu.VMEM((7, UB, 256), BF16),
            pltpu.VMEM((UB, 256), BF16),
            pltpu.VMEM((ROWS, 256), BF16),
            pltpu.VMEM((ROWS, 128), BF16),
            pltpu.VMEM((7, UB, 128), BF16),
            pltpu.VMEM((UB, 128), BF16),
            pltpu.VMEM((ROWS, 128), BF16),
        ] + [block] * 14 + [
            pltpu.SemaphoreType.DMA((12,)),
            pltpu.SemaphoreType.DMA((N_COPIES,)),
            pltpu.SemaphoreType.DMA((N_COPIES,)),
        ],
        compiler_params=pltpu.CompilerParams(
            collective_id=0, has_side_effects=True, vmem_limit_bytes=60 * 2**20
        ),
    )(tokens, norm_gain.reshape(1, WIDTH), route_ids.T, route_gates.T, w_gate, w_up, w_down, a_factors, b_factors)


def solution(mesh):
    placed = (
        P("wide", "fsdp"),
        P(),
        P("wide", None),
        P("wide", None),
        P(None, "fsdp", None),
        P(None, "fsdp", None),
        P(None, "fsdp", None),
        P(None, None, "wide", "fsdp"),
        P(None, None, "wide", "fsdp"),
    )
    return jax.shard_map(
        per_device, mesh=mesh, in_specs=placed, out_specs=P("wide", "fsdp"), check_vma=False
    )
```

```python
import functools

import jax
import jax.numpy as jnp
from jax import lax
from jax.experimental import pallas as pl
from jax.experimental.pallas import tpu as pltpu
from jax.sharding import PartitionSpec as P

F32, BF16 = jnp.float32, jnp.bfloat16
MESH = pl.DeviceIdType.MESH
ROWS, COLS, HID, WIDTH = 256, 512, 192, 4096
HALF, QUART = 128, 64
UB = 32
SHIFT = 32


def dot_nt(a, b):
    return lax.dot_general(a, b, (((1,), (1,)), ((), ())), preferred_element_type=F32)


def dot_nn(a, b):
    return jnp.dot(a, b, preferred_element_type=F32)


def iota(shape, dim):
    return lax.broadcasted_iota(jnp.int32, shape, dim)


def body(
    x_hbm, gain_hbm, ids_hbm, gates_hbm, wg_hbm, wu_hbm, wd_hbm, a_hbm, b_hbm, out_hbm,
    x_ref, gain_ref, ids_ref, gates_ref, a_ref, b_ref, w_in, w_down, pack_a, pack_b, fac_a, fac_b, fa, fb, b_exp, bd_t, ad_c, mixed,
    xb, acc, sq, hid,
    u_part, u_in, u_blk, u_all, v_part, v_in, v_blk, v_all,
    s1, s2p, s2m, s3, s4p, s4m, s5, r1, r2p, r2m, r3, r4p, r4m, r5,
    o_buf, r6p, r6m, wsem, ssem, rsem,
):
    w = lax.axis_index("wide")
    f = lax.axis_index("fsdp")
    zh, xx, core = w // 8, (w // 2) % 4, w % 2
    y, z = f // 2, f % 2

    def fs(dy, flip):
        zz = 1 - z if flip else z
        return ((y + dy) % 4) * 2 + zz

    def wide_at(dzh, dx, dcore):
        return (((zh + dzh) % 4) * 4 + (xx + dx) % 4) * 2 + (core + dcore) % 2

    up, down, across = (w, fs(1, False)), (w, fs(3, False)), (w, fs(0, True))
    count = [0]

    def remote(src, dst, dev):
        i = count[0]
        count[0] += 1
        return pltpu.make_async_remote_copy(
            src_ref=src, dst_ref=dst, send_sem=ssem.at[i], recv_sem=rsem.at[i],
            device_id=dev, device_id_type=MESH,
        )

    small = [
        pltpu.make_async_copy(src, dst, wsem.at[6 + i])
        for i, (src, dst) in enumerate((
            (a_hbm, a_ref), (b_hbm, b_ref), (x_hbm, x_ref),
            (gain_hbm, gain_ref), (ids_hbm, ids_ref), (gates_hbm, gates_ref),
        ))
    ]
    for c in small:
        c.start()
    loads = []
    for e in range(2):
        for j, (ref, dst) in enumerate(((wg_hbm, w_in.at[pl.ds(e * HID, HID)]),
                                        (wu_hbm, w_in.at[pl.ds((2 + e) * HID, HID)]),
                                        (wd_hbm, w_down.at[pl.ds(e * HID, HID)]))):
            c = pltpu.make_async_copy(ref.at[e], dst, wsem.at[e * 3 + j])
            c.start()
            loads.append(c)

    peers = [(wide_at(d // 2, 0, d % 2), f) for d in range(1, 8)] + [(wide_at(0, d, 0), f) for d in (1, 2, 3)]
    peers += [(w, (f + i) % 8) for i in range(1, 8)]
    barrier = pltpu.get_barrier_semaphore()
    for p in peers:
        pl.semaphore_signal(barrier, inc=1, device_id=p, device_id_type=MESH)

    small[0].wait()
    for e in range(2):
        for p in range(2):
            pack_a[e * 4 + p * 2:e * 4 + p * 2 + 2, :] = a_ref[e, p]
    fac_a[0, 0, 0] = jnp.concatenate([pack_a[:, 0:256], pack_a[:, 256:512]], axis=0).astype(BF16)

    def pack_second():
        pack_b[...] = jnp.zeros_like(pack_b)
        for e in range(2):
            for p in range(2):
                pack_b[e * 4 + p * 2:e * 4 + p * 2 + 2, 0:192] = b_ref[e, p]
            for h in range(2):
                pack_b[h * 4 + e * 2:h * 4 + e * 2 + 2, 256:512] = a_ref[e, 2, :, h * 256:(h + 1) * 256]
            pack_b[e * 2:e * 2 + 2, 512:704] = b_ref[e, 2]
        fac_b[0, 0, 0] = jnp.concatenate([pack_b[:, 0:384], pack_b[:, 384:768]], axis=0).astype(BF16)

    for c in small[1:]:
        c.wait()
    pl.semaphore_wait(barrier, len(peers))

    def half(ref, h):
        return ref.at[pl.ds(h * HALF, HALF)]

    def quart(ref, h, q):
        return ref.at[pl.ds(h * HALF + q * QUART, QUART)]

    near = [(dz, dc) for dc in (0, 1) for dz in (2, 1, 3, 0) if dz or dc]

    def factor_copies(fac):
        by_z = [
            remote(fac.at[0, 0, 0], fac.at[0, dc, (4 - dz) % 4], (wide_at(dz, 0, dc), f)) for dz, dc in near
        ]
        by_x = [remote(fac.at[0], fac.at[4 - d], (wide_at(0, d, 0), f)) for d in (2, 1, 3)]
        return by_z, by_x

    az, ax = factor_copies(fac_a)
    bz, bx = factor_copies(fac_b)
    tok = []
    for h in range(2):
        t = {}
        t["up"] = remote(half(x_ref, h), half(xb.at[0], h), up)
        t["down"] = remote(half(x_ref, h), half(xb.at[1], h), down)
        t["across"] = remote(half(x_ref, h), half(xb.at[2], h), across)
        t["far0"] = remote(quart(xb.at[0], h, 0), quart(xb.at[3], h, 0), up)
        t["far1"] = remote(quart(xb.at[1], h, 1), quart(xb.at[3], h, 1), down)
        t["dup"] = remote(half(xb.at[2], h), half(xb.at[4], h), up)
        t["ddown"] = remote(half(xb.at[2], h), half(xb.at[5], h), down)
        t["dfar"] = remote(half(xb.at[3], h), half(xb.at[6], h), across)
        tok.append(t)
    src = [fs(3, False), fs(1, False), fs(0, True), fs(2, False), fs(3, True), fs(1, True), fs(2, True)]
    other = [(w, (f + i) % 8) for i in range(1, 8)]
    mine = pl.ds(pl.multiple_of(f * UB, UB), UB)

    def rows_of(i):
        return pl.ds(pl.multiple_of(((f + i) % 8) * UB, UB), UB)

    u_rs = [remote(u_part.at[rows_of(i)], u_in.at[i - 1], other[i - 1]) for i in range(1, 8)]
    u_ag = [remote(u_blk, u_all.at[mine], other[i - 1]) for i in range(1, 8)]
    v_rs = [remote(v_part.at[rows_of(i)], v_in.at[i - 1], other[i - 1]) for i in range(1, 8)]
    v_ag = [remote(v_blk, v_all.at[mine], other[i - 1]) for i in range(1, 8)]
    red = []
    for h in range(2):
        t = {}
        t["t1"] = remote(half(s1, h), half(r1, h), across)
        kept_p = pl.ds(h * HALF, HALF - h * SHIFT)
        kept_m = pl.ds(h * HALF + h * SHIFT, HALF - h * SHIFT)
        t["t2p"] = remote(s2p.at[kept_p], r2m.at[kept_p], up)
        t["t2m"] = remote(s2m.at[kept_m], r2p.at[kept_m], down)
        if h == 1:
            t["t6p"] = remote(s2p.at[pl.ds(ROWS - SHIFT, SHIFT)], r6p, across)
            t["t6m"] = remote(s2m.at[pl.ds(HALF, SHIFT)], r6m, across)
        t["t3p"] = remote(quart(s3, h, 0), quart(r3, h, 0), up)
        t["t3m"] = remote(quart(s3, h, 1), quart(r3, h, 1), down)
        t["t4p0"] = remote(quart(s4p, h, 0), quart(r4m, h, 0), up)
        t["t4p1"] = remote(quart(s4p, h, 1), quart(r4m, h, 1), up)
        t["t4m0"] = remote(quart(s4m, h, 0), quart(r4p, h, 0), down)
        t["t4m1"] = remote(quart(s4m, h, 1), quart(r4p, h, 1), down)
        t["t5"] = remote(half(s5, h), half(r5, h), across)
        red.append(t)

    def start(h, *names):
        for n in names:
            tok[h][n].start()

    def got(h, *names):
        for n in names:
            tok[h][n].wait_recv()

    def rstart(h, *names):
        for n in names:
            red[h][n].start()

    def rgot(h, *names):
        for n in names:
            red[h][n].wait_recv()

    def scaled(ref, owner):
        lanes = pl.ds(pl.multiple_of(owner * COLS, COLS), COLS)
        v = ref[...].astype(F32)
        s = v * v
        s = (s[:, 0:128] + s[:, 128:256]) + (s[:, 256:384] + s[:, 384:512])
        return (v * gain_ref[:, lanes]).astype(BF16), s, lanes

    def project(ref, owner, first=False):
        xg, s, lanes = scaled(ref, owner)
        prod = dot_nt(xg, w_in[:, lanes])
        if first:
            acc[...] = prod
            sq[...] = s
        else:
            acc[...] += prod
            sq[...] += s

    def block(rows, owner):
        lanes = pl.ds(pl.multiple_of(owner * COLS, COLS), COLS)
        return dot_nn(hid[rows, :], w_down[:, lanes])

    def activate(h):
        rows = pl.ds(h * HALF, HALF)
        mean = jnp.sum(sq[rows, :], axis=-1, keepdims=True) * (1.0 / WIDTH)
        scale = lax.rsqrt(mean + 1e-06)
        pre = (acc[rows, :] + dot_nn(u_all[rows, :], b_exp[...])) * scale
        g, u = pre[:, 0:2 * HID], pre[:, 2 * HID:4 * HID]
        hid[rows, :] = (g / (1.0 + jnp.exp(-g)) * u * mixed[rows, :]).astype(BF16)

    def mix_rows():
        ids, gates = ids_ref[...], gates_ref[...]
        mix = [jnp.sum(jnp.where(ids == e, gates, 0.0), axis=0, keepdims=True) for e in range(2)]
        r = iota((8, ROWS), 0)
        mix = jnp.where(r == 0, mix[0], jnp.where(r == 1, mix[1], 0.0))
        pick = (iota((8, 2 * HID), 0) == iota((8, 2 * HID), 1) // HID).astype(F32)
        mixed[...] = lax.dot_general(
            mix, pick, (((0,), (0,)), ((), ())), precision=lax.Precision.HIGHEST, preferred_element_type=F32
        )

    def to_block(dst, rows, owner):
        dst[rows, :] = block(rows, owner).astype(BF16)

    def rows_half(h):
        return pl.ds(h * HALF, HALF)

    def send_far(h):
        rows = rows_half(h)
        rgot(h, "t1")
        s3[rows, :] = (s3[rows, :].astype(F32) + r1[rows, :].astype(F32)).astype(BF16)
        rstart(h, "t3p", "t3m")

    def send_across(h):
        rows = rows_half(h)
        rgot(h, "t2p", "t2m")
        kept_p = pl.ds(h * HALF, HALF - h * SHIFT)
        kept_m = pl.ds(h * HALF + h * SHIFT, HALF - h * SHIFT)
        total = s5[rows, :].astype(F32)
        low, high = r2m[kept_p, :].astype(F32), r2p[kept_m, :].astype(F32)
        if h == 1:
            none = jnp.zeros((SHIFT, COLS), F32)
            low, high = jnp.concatenate([low, none], axis=0), jnp.concatenate([none, high], axis=0)
        s5[rows, :] = (total + low + high).astype(BF16)
        rstart(h, "t5")

    def send_near(h):
        q0, q1 = pl.ds(h * HALF, QUART), pl.ds(h * HALF + QUART, QUART)
        rgot(h, "t3p")
        s4p[q0, :] = (s4p[q0, :].astype(F32) + r3[q0, :].astype(F32)).astype(BF16)
        rstart(h, "t4p0")
        rgot(h, "t3m")
        s4m[q1, :] = (s4m[q1, :].astype(F32) + r3[q1, :].astype(F32)).astype(BF16)
        rstart(h, "t4m1")

    stores = [pltpu.make_async_copy(half(o_buf, h), half(out_hbm, h), wsem.at[12 + h]) for h in range(2)]

    def finish(h):
        rows = rows_half(h)
        rgot(h, "t5", "t4p1", "t4m0", "t4p0", "t4m1")
        part = acc[rows, 0:COLS] + r4p[rows, :].astype(F32) + r4m[rows, :].astype(F32) + r5[rows, :].astype(F32)
        o_buf[rows, :] = part.astype(BF16)
        stores[h].start()

    def exchange_sum(part, arrived, blk, whole, rs, ag):
        total = part[mine, :].astype(F32)
        for i in range(7):
            rs[i].wait_recv()
            total = total + arrived[i].astype(F32)
        blk[...] = total.astype(BF16)
        whole[mine, :] = total.astype(BF16)
        for c in ag:
            c.start()

    def over_x(by_z, by_x):
        for c in by_z:
            c.wait_recv()
        for c in by_x:
            c.start()

    def unpack(fac, whole, width):
        def step(i, carry):
            rows = pl.ds(pl.multiple_of(i * 16, 16), 16)
            two = [fac[i // 4, (i // 2) % 2, (i % 2) * 2 + k].astype(F32) for k in range(2)]
            whole[rows, 0:width] = jnp.concatenate([two[0][0:8], two[1][0:8]], axis=0).astype(BF16)
            whole[rows, width:2 * width] = jnp.concatenate([two[0][8:16], two[1][8:16]], axis=0).astype(BF16)
            return carry

        lax.fori_loop(0, 16, step, 0)

    def prepare():
        rep = (iota((256, 4 * HID), 0) == iota((256, 4 * HID), 1) % HID).astype(BF16)
        k, j = iota((256, 4 * HID), 0), iota((256, 4 * HID), 1) // HID
        keep = ((k % 8) // 4 + 2 * ((k % 4) // 2)) == j
        b_exp[...] = jnp.where(keep, 2.0 * dot_nn(fb[:, 0:256], rep), 0.0).astype(BF16)
        r, k = iota((128, 256), 0), iota((128, 256), 1)
        slot = (r // 4) * 8 + r % 4
        sel0, sel1 = (k == slot).astype(BF16), (k == slot + 4).astype(BF16)
        bd = dot_nn(sel0, fb[:, 512:768]).astype(BF16)
        r, j = iota((128, 2 * HID), 0), iota((128, 2 * HID), 1) // HID
        bd_t[...] = jnp.where((r % 4) // 2 == j, dot_nn(bd, rep[:, 0:2 * HID]), 0.0).astype(BF16)
        ad_c[:, 0:256] = (2.0 * dot_nn(sel0, fb[:, 256:512])).astype(BF16)
        ad_c[:, 256:512] = (2.0 * dot_nn(sel1, fb[:, 256:512])).astype(BF16)

    for c in az:
        c.start()
    start(0, "up", "down", "across")
    start(1, "up", "down", "across")
    pack_second()
    for c in loads:
        c.wait()
    project(x_ref, f, True)
    mix_rows()
    over_x(az, ax)
    for c in bz:
        c.start()
    got(0, "up")
    start(0, "far0")
    got(0, "down")
    start(0, "far1")
    got(1, "up")
    start(1, "far0")
    got(1, "down")
    start(1, "far1")
    for c in ax:
        c.wait_recv()
    unpack(fac_a, fa, 256)
    xg, _, _ = scaled(x_ref, f)
    u_part[...] = dot_nt(xg, fa[...]).astype(BF16)
    for c in u_rs:
        c.start()
    got(0, "across")
    start(0, "dup", "ddown")
    got(1, "across")
    start(1, "dup", "ddown")
    got(0, "far0", "far1")
    start(0, "dfar")
    over_x(bz, bx)
    got(1, "far0", "far1")
    start(1, "dfar")
    project(xb.at[0], src[0])
    exchange_sum(u_part, u_in, u_blk, u_all, u_rs, u_ag)
    project(xb.at[1], src[1])
    project(xb.at[2], src[2])
    project(xb.at[3], src[3])
    for c in bx:
        c.wait_recv()
    unpack(fac_b, fb, 384)
    prepare()
    got(0, "dup", "ddown")
    got(1, "dup", "ddown")
    project(xb.at[4], src[4])
    project(xb.at[5], src[5])
    got(0, "dfar")
    got(1, "dfar")
    project(xb.at[6], src[6])
    for c in u_ag:
        c.wait_recv()
    both = pl.ds(0, ROWS)
    for h in range(2):
        activate(h)
        to_block(s2p, rows_half(h), fs(1, True))
        rstart(h, "t2p")
        to_block(s2m, rows_half(h), fs(3, True))
        rstart(h, "t2m")
        to_block(s1, rows_half(h), fs(2, True))
        rstart(h, "t1")
        if h == 1:
            rstart(1, "t6p", "t6m")
    v_part[...] = dot_nt(hid[...], bd_t[...]).astype(BF16)
    for c in v_rs:
        c.start()
    to_block(s3, both, fs(2, False))
    to_block(s4p, both, fs(1, False))
    to_block(s4m, both, fs(3, False))
    send_far(0)
    rstart(0, "t4p1", "t4m0")
    to_block(s5, both, fs(0, True))
    acc[:, 0:COLS] = block(both, f)
    send_across(0)
    send_far(1)
    exchange_sum(v_part, v_in, v_blk, v_all, v_rs, v_ag)
    rgot(1, "t6p", "t6m")
    last, lead = pl.ds(ROWS - SHIFT, SHIFT), pl.ds(HALF, SHIFT)
    s4p[last, :] = (s4p[last, :].astype(F32) + r6p[...].astype(F32)).astype(BF16)
    s4m[lead, :] = (s4m[lead, :].astype(F32) + r6m[...].astype(F32)).astype(BF16)
    rstart(1, "t4p1", "t4m0")
    send_near(0)
    send_across(1)
    send_near(1)
    for c in v_ag:
        c.wait_recv()
    acc[:, 0:COLS] += dot_nn(v_all[...], ad_c[...])
    finish(0)
    finish(1)
    for c in stores:
        c.wait()
    for c in az + ax + bz + bx + u_rs + u_ag + v_rs + v_ag:
        c.wait_send()
    for t in tok + red:
        for c in t.values():
            c.wait_send()


N_COPIES = 20 + 16 + 28 + 20 + 2


def per_device(tokens, norm_gain, route_ids, route_gates, w_gate, w_up, w_down, a_factors, b_factors):
    hbm = pl.BlockSpec(memory_space=pl.ANY)
    block = pltpu.VMEM((ROWS, COLS), BF16)
    return pl.pallas_call(
        body,
        out_shape=jax.ShapeDtypeStruct((ROWS, COLS), BF16),
        in_specs=[hbm] * 9,
        out_specs=hbm,
        scratch_shapes=[
            pltpu.VMEM((ROWS, COLS), BF16),
            pltpu.VMEM((1, WIDTH), F32),
            pltpu.VMEM((2, ROWS), jnp.int32),
            pltpu.VMEM((2, ROWS), F32),
            pltpu.VMEM((2, 3, 2, COLS), F32),
            pltpu.VMEM((2, 3, 2, HID), F32),
            pltpu.VMEM((4 * HID, WIDTH), BF16),
            pltpu.VMEM((2 * HID, WIDTH), BF16),
            pltpu.VMEM((8, 512), F32),
            pltpu.VMEM((8, 768), F32),
            pltpu.VMEM((4, 2, 4, 16, 256), BF16),
            pltpu.VMEM((4, 2, 4, 16, 384), BF16),
            pltpu.VMEM((256, 512), BF16),
            pltpu.VMEM((256, 768), BF16),
            pltpu.VMEM((256, 4 * HID), BF16),
            pltpu.VMEM((128, 2 * HID), BF16),
            pltpu.VMEM((128, COLS), BF16),
            pltpu.VMEM((ROWS, 2 * HID), F32),
            pltpu.VMEM((7, ROWS, COLS), BF16),
            pltpu.VMEM((ROWS, 4 * HID), F32),
            pltpu.VMEM((ROWS, 128), F32),
            pltpu.VMEM((ROWS, 2 * HID), BF16),
            pltpu.VMEM((ROWS, 256), BF16),
            pltpu.VMEM((7, UB, 256), BF16),
            pltpu.VMEM((UB, 256), BF16),
            pltpu.VMEM((ROWS, 256), BF16),
            pltpu.VMEM((ROWS, 128), BF16),
            pltpu.VMEM((7, UB, 128), BF16),
            pltpu.VMEM((UB, 128), BF16),
            pltpu.VMEM((ROWS, 128), BF16),
        ] + [block] * 15 + [
            pltpu.VMEM((SHIFT, COLS), BF16),
            pltpu.VMEM((SHIFT, COLS), BF16),
            pltpu.SemaphoreType.DMA((14,)),
            pltpu.SemaphoreType.DMA((N_COPIES,)),
            pltpu.SemaphoreType.DMA((N_COPIES,)),
        ],
        compiler_params=pltpu.CompilerParams(
            collective_id=0, has_side_effects=True, vmem_limit_bytes=60 * 2**20
        ),
    )(tokens, norm_gain.reshape(1, WIDTH), route_ids.T, route_gates.T, w_gate, w_up, w_down, a_factors, b_factors)


def solution(mesh):
    placed = (
        P("wide", "fsdp"),
        P(),
        P("wide", None),
        P("wide", None),
        P(None, "fsdp", None),
        P(None, "fsdp", None),
        P(None, "fsdp", None),
        P(None, None, "wide", "fsdp"),
        P(None, None, "wide", "fsdp"),
    )
    return jax.shard_map(
        per_device, mesh=mesh, in_specs=placed, out_specs=P("wide", "fsdp"), check_vma=False
    )
```

```python
import functools

import jax
import jax.numpy as jnp
from jax import lax
from jax.experimental import pallas as pl
from jax.experimental.pallas import tpu as pltpu
from jax.sharding import PartitionSpec as P

F32, BF16 = jnp.float32, jnp.bfloat16
MESH = pl.DeviceIdType.MESH
ROWS, COLS, HID, WIDTH = 256, 512, 192, 4096
HALF, QUART = 128, 64
UB = 32
SHIFT = 48


def dot_nt(a, b):
    return lax.dot_general(a, b, (((1,), (1,)), ((), ())), preferred_element_type=F32)


def dot_nn(a, b):
    return jnp.dot(a, b, preferred_element_type=F32)


def iota(shape, dim):
    return lax.broadcasted_iota(jnp.int32, shape, dim)


def body(
    x_hbm, gain_hbm, ids_hbm, gates_hbm, wg_hbm, wu_hbm, wd_hbm, a_hbm, b_hbm, out_hbm,
    x_ref, gain_ref, ids_ref, gates_ref, a_ref, b_ref, w_in, w_down, pack_a, pack_b, fac_a, fac_b, fa, fb, b_exp, bd_t, ad_c, mixed,
    xb, acc, sq, hid,
    u_part, u_in, u_blk, u_all, v_part, v_in, v_blk, v_all,
    s1, s2p, s2m, s3, s4p, s4m, s5, r1, r2p, r2m, r3, r4p, r4m, r5,
    o_buf, r6p, r6m, wsem, ssem, rsem,
):
    w = lax.axis_index("wide")
    f = lax.axis_index("fsdp")
    zh, xx, core = w // 8, (w // 2) % 4, w % 2
    y, z = f // 2, f % 2

    def fs(dy, flip):
        zz = 1 - z if flip else z
        return ((y + dy) % 4) * 2 + zz

    def wide_at(dzh, dx, dcore):
        return (((zh + dzh) % 4) * 4 + (xx + dx) % 4) * 2 + (core + dcore) % 2

    up, down, across = (w, fs(1, False)), (w, fs(3, False)), (w, fs(0, True))
    count = [0]

    def remote(src, dst, dev):
        i = count[0]
        count[0] += 1
        return pltpu.make_async_remote_copy(
            src_ref=src, dst_ref=dst, send_sem=ssem.at[i], recv_sem=rsem.at[i],
            device_id=dev, device_id_type=MESH,
        )

    small = [
        pltpu.make_async_copy(src, dst, wsem.at[6 + i])
        for i, (src, dst) in enumerate((
            (a_hbm, a_ref), (b_hbm, b_ref), (x_hbm, x_ref),
            (gain_hbm, gain_ref), (ids_hbm, ids_ref), (gates_hbm, gates_ref),
        ))
    ]
    small[0].start()

    peers = [(wide_at(d // 2, 0, d % 2), f) for d in range(1, 8)] + [(wide_at(0, d, 0), f) for d in (1, 2, 3)]
    peers += [(w, (f + i) % 8) for i in range(1, 8)]
    barrier = pltpu.get_barrier_semaphore()
    for p in peers:
        pl.semaphore_signal(barrier, inc=1, device_id=p, device_id_type=MESH)

    for c in small[1:]:
        c.start()
    loads = []
    for e in range(2):
        for j, (ref, dst) in enumerate(((wg_hbm, w_in.at[pl.ds(e * HID, HID)]),
                                        (wu_hbm, w_in.at[pl.ds((2 + e) * HID, HID)]),
                                        (wd_hbm, w_down.at[pl.ds(e * HID, HID)]))):
            c = pltpu.make_async_copy(ref.at[e], dst, wsem.at[e * 3 + j])
            c.start()
            loads.append(c)

    small[0].wait()
    for e in range(2):
        for p in range(2):
            pack_a[e * 4 + p * 2:e * 4 + p * 2 + 2, :] = a_ref[e, p]
    fac_a[0, 0, 0] = jnp.concatenate([pack_a[:, 0:256], pack_a[:, 256:512]], axis=0).astype(BF16)

    def pack_second():
        pack_b[...] = jnp.zeros_like(pack_b)
        for e in range(2):
            for p in range(2):
                pack_b[e * 4 + p * 2:e * 4 + p * 2 + 2, 0:192] = b_ref[e, p]
            for h in range(2):
                pack_b[h * 4 + e * 2:h * 4 + e * 2 + 2, 256:512] = a_ref[e, 2, :, h * 256:(h + 1) * 256]
            pack_b[e * 2:e * 2 + 2, 512:704] = b_ref[e, 2]
        fac_b[0, 0, 0] = jnp.concatenate([pack_b[:, 0:384], pack_b[:, 384:768]], axis=0).astype(BF16)

    pl.semaphore_wait(barrier, len(peers))

    def half(ref, h):
        return ref.at[pl.ds(h * HALF, HALF)]

    def quart(ref, h, q):
        return ref.at[pl.ds(h * HALF + q * QUART, QUART)]

    near = [(dz, dc) for dz in (2, 1, 3, 0) for dc in (0, 1) if dz or dc]

    def factor_copies(fac):
        by_z = [
            remote(fac.at[0, 0, 0], fac.at[0, (4 - dz) % 4, dc], (wide_at(dz, 0, dc), f)) for dz, dc in near
        ]
        by_x = [remote(fac.at[0], fac.at[4 - d], (wide_at(0, d, 0), f)) for d in (2, 1, 3)]
        return by_z, by_x

    az, _ = factor_copies(fac_a)
    ax_of = {
        slot: [remote(fac_a.at[0, slot], fac_a.at[4 - d, slot], (wide_at(0, d, 0), f)) for d in (2, 1, 3)]
        for slot in (0, 1, 3, 2)
    }
    ax = [c for slot in (0, 1, 3, 2) for c in ax_of[slot]]
    bz, bx = factor_copies(fac_b)
    tok = []
    for h in range(2):
        t = {}
        t["up"] = remote(half(x_ref, h), half(xb.at[0], h), up)
        t["down"] = remote(half(x_ref, h), half(xb.at[1], h), down)
        t["across"] = remote(half(x_ref, h), half(xb.at[2], h), across)
        t["far0"] = remote(quart(xb.at[0], h, 0), quart(xb.at[3], h, 0), up)
        t["far1"] = remote(quart(xb.at[1], h, 1), quart(xb.at[3], h, 1), down)
        t["dup"] = remote(half(xb.at[2], h), half(xb.at[4], h), up)
        t["ddown"] = remote(half(xb.at[2], h), half(xb.at[5], h), down)
        t["dfar"] = remote(half(xb.at[3], h), half(xb.at[6], h), across)
        tok.append(t)
    src = [fs(3, False), fs(1, False), fs(0, True), fs(2, False), fs(3, True), fs(1, True), fs(2, True)]
    other = [(w, (f + i) % 8) for i in range(1, 8)]
    mine = pl.ds(pl.multiple_of(f * UB, UB), UB)

    far_first = (2, 4, 3, 1, 5, 0, 6)

    def rows_of(i):
        return pl.ds(pl.multiple_of(((f + i) % 8) * UB, UB), UB)

    u_rs = [remote(u_part.at[rows_of(i)], u_in.at[i - 1], other[i - 1]) for i in range(1, 8)]
    u_ag = [remote(u_blk, u_all.at[mine], other[i - 1]) for i in range(1, 8)]
    v_rs = [remote(v_part.at[rows_of(i)], v_in.at[i - 1], other[i - 1]) for i in range(1, 8)]
    v_ag = [remote(v_blk, v_all.at[mine], other[i - 1]) for i in range(1, 8)]
    red = []
    for h in range(2):
        t = {}
        t["t1"] = remote(half(s1, h), half(r1, h), across)
        kept_p = pl.ds(h * HALF, HALF - h * SHIFT)
        kept_m = pl.ds(h * HALF + h * SHIFT, HALF - h * SHIFT)
        t["t2p"] = remote(s2p.at[kept_p], r2m.at[kept_p], up)
        t["t2m"] = remote(s2m.at[kept_m], r2p.at[kept_m], down)
        if h == 1:
            t["t6p"] = remote(s2p.at[pl.ds(ROWS - SHIFT, SHIFT)], r6p, across)
            t["t6m"] = remote(s2m.at[pl.ds(HALF, SHIFT)], r6m, across)
        t["t3p"] = remote(quart(s3, h, 0), quart(r3, h, 0), up)
        t["t3m"] = remote(quart(s3, h, 1), quart(r3, h, 1), down)
        t["t4p0"] = remote(quart(s4p, h, 0), quart(r4m, h, 0), up)
        t["t4p1"] = remote(quart(s4p, h, 1), quart(r4m, h, 1), up)
        t["t4m0"] = remote(quart(s4m, h, 0), quart(r4p, h, 0), down)
        t["t4m1"] = remote(quart(s4m, h, 1), quart(r4p, h, 1), down)
        t["t5"] = remote(half(s5, h), half(r5, h), across)
        red.append(t)

    def start(h, *names):
        for n in names:
            tok[h][n].start()

    def got(h, *names):
        for n in names:
            tok[h][n].wait_recv()

    def rstart(h, *names):
        for n in names:
            red[h][n].start()

    def rgot(h, *names):
        for n in names:
            red[h][n].wait_recv()

    def scaled(ref, owner):
        lanes = pl.ds(pl.multiple_of(owner * COLS, COLS), COLS)
        v = ref[...].astype(F32)
        s = v * v
        s = (s[:, 0:128] + s[:, 128:256]) + (s[:, 256:384] + s[:, 384:512])
        return (v * gain_ref[:, lanes]).astype(BF16), s, lanes

    def project(ref, owner, first=False):
        xg, s, lanes = scaled(ref, owner)
        prod = dot_nt(xg, w_in[:, lanes])
        if first:
            acc[...] = prod
            sq[...] = s
        else:
            acc[...] += prod
            sq[...] += s

    def block(rows, owner):
        lanes = pl.ds(pl.multiple_of(owner * COLS, COLS), COLS)
        return dot_nn(hid[rows, :], w_down[:, lanes])

    def activate(h):
        rows = pl.ds(h * HALF, HALF)
        mean = jnp.sum(sq[rows, :], axis=-1, keepdims=True) * (1.0 / WIDTH)
        scale = lax.rsqrt(mean + 1e-06)
        pre = (acc[rows, :] + dot_nn(u_all[rows, :], b_exp[...])) * scale
        g, u = pre[:, 0:2 * HID], pre[:, 2 * HID:4 * HID]
        hid[rows, :] = (g / (1.0 + jnp.exp(-g)) * u * mixed[rows, :]).astype(BF16)

    def mix_rows():
        ids, gates = ids_ref[...], gates_ref[...]
        mix = [jnp.sum(jnp.where(ids == e, gates, 0.0), axis=0, keepdims=True) for e in range(2)]
        r = iota((8, ROWS), 0)
        mix = jnp.where(r == 0, mix[0], jnp.where(r == 1, mix[1], 0.0))
        pick = (iota((8, 2 * HID), 0) == iota((8, 2 * HID), 1) // HID).astype(F32)
        mixed[...] = lax.dot_general(
            mix, pick, (((0,), (0,)), ((), ())), precision=lax.Precision.HIGHEST, preferred_element_type=F32
        )

    def to_block(dst, rows, owner):
        dst[rows, :] = block(rows, owner).astype(BF16)

    def rows_half(h):
        return pl.ds(h * HALF, HALF)

    def send_far(h):
        rows = rows_half(h)
        rgot(h, "t1")
        s3[rows, :] = (s3[rows, :].astype(F32) + r1[rows, :].astype(F32)).astype(BF16)
        rstart(h, "t3p", "t3m")

    def send_across(h):
        rows = rows_half(h)
        rgot(h, "t2p", "t2m")
        kept_p = pl.ds(h * HALF, HALF - h * SHIFT)
        kept_m = pl.ds(h * HALF + h * SHIFT, HALF - h * SHIFT)
        total = s5[rows, :].astype(F32)
        low, high = r2m[kept_p, :].astype(F32), r2p[kept_m, :].astype(F32)
        if h == 1:
            none = jnp.zeros((SHIFT, COLS), F32)
            low, high = jnp.concatenate([low, none], axis=0), jnp.concatenate([none, high], axis=0)
        s5[rows, :] = (total + low + high).astype(BF16)
        rstart(h, "t5")

    def send_near(h):
        q0, q1 = pl.ds(h * HALF, QUART), pl.ds(h * HALF + QUART, QUART)
        rgot(h, "t3p")
        s4p[q0, :] = (s4p[q0, :].astype(F32) + r3[q0, :].astype(F32)).astype(BF16)
        rstart(h, "t4p0")
        rgot(h, "t3m")
        s4m[q1, :] = (s4m[q1, :].astype(F32) + r3[q1, :].astype(F32)).astype(BF16)
        rstart(h, "t4m1")

    stores = [pltpu.make_async_copy(half(o_buf, h), half(out_hbm, h), wsem.at[12 + h]) for h in range(2)]

    def finish(h):
        rows = rows_half(h)
        rgot(h, "t5", "t4p1", "t4m0", "t4p0", "t4m1")
        part = acc[rows, 0:COLS] + r4p[rows, :].astype(F32) + r4m[rows, :].astype(F32) + r5[rows, :].astype(F32)
        o_buf[rows, :] = part.astype(BF16)
        stores[h].start()

    def exchange_sum(part, arrived, blk, whole, rs, ag):
        total = part[mine, :].astype(F32)
        for i in range(7):
            rs[i].wait_recv()
            total = total + arrived[i].astype(F32)
        blk[...] = total.astype(BF16)
        whole[mine, :] = total.astype(BF16)
        for i in far_first:
            ag[i].start()

    def over_x(by_z, by_x):
        for c in by_z:
            c.wait_recv()
        for c in by_x:
            c.start()

    def unpack(fac, whole, width):
        def step(i, carry):
            rows = pl.ds(pl.multiple_of(i * 16, 16), 16)
            two = [fac[i // 4, i % 4, k].astype(F32) for k in range(2)]
            whole[rows, 0:width] = jnp.concatenate([two[0][0:8], two[1][0:8]], axis=0).astype(BF16)
            whole[rows, width:2 * width] = jnp.concatenate([two[0][8:16], two[1][8:16]], axis=0).astype(BF16)
            return carry

        lax.fori_loop(0, 16, step, 0)

    def prepare():
        rep = (iota((256, 4 * HID), 0) == iota((256, 4 * HID), 1) % HID).astype(BF16)
        k, j = iota((256, 4 * HID), 0), iota((256, 4 * HID), 1) // HID
        keep = ((k % 8) // 4 + 2 * ((k % 4) // 2)) == j
        b_exp[...] = jnp.where(keep, 2.0 * dot_nn(fb[:, 0:256], rep), 0.0).astype(BF16)
        r, k = iota((128, 256), 0), iota((128, 256), 1)
        slot = (r // 4) * 8 + r % 4
        sel0, sel1 = (k == slot).astype(BF16), (k == slot + 4).astype(BF16)
        bd = dot_nn(sel0, fb[:, 512:768]).astype(BF16)
        r, j = iota((128, 2 * HID), 0), iota((128, 2 * HID), 1) // HID
        bd_t[...] = jnp.where((r % 4) // 2 == j, dot_nn(bd, rep[:, 0:2 * HID]), 0.0).astype(BF16)
        ad_c[:, 0:256] = (2.0 * dot_nn(sel0, fb[:, 256:512])).astype(BF16)
        ad_c[:, 256:512] = (2.0 * dot_nn(sel1, fb[:, 256:512])).astype(BF16)

    for c in az:
        c.start()
    for c in small[1:]:
        c.wait()
    start(0, "up", "down", "across")
    start(1, "up", "down", "across")
    pack_second()
    for c in loads:
        c.wait()
    project(x_ref, f, True)
    mix_rows()
    for slot in (0, 1, 3, 2):
        for c, (dz, dc) in zip(az, near):
            if (4 - dz) % 4 == slot:
                c.wait_recv()
        for c in ax_of[slot]:
            c.start()
    for c in bz:
        c.start()
    got(0, "up")
    start(0, "far0")
    got(0, "down")
    start(0, "far1")
    got(1, "up")
    start(1, "far0")
    got(1, "down")
    start(1, "far1")
    for c in ax:
        c.wait_recv()
    unpack(fac_a, fa, 256)
    xg, _, _ = scaled(x_ref, f)
    u_part[...] = dot_nt(xg, fa[...]).astype(BF16)
    for i in far_first:
        u_rs[i].start()
    got(0, "across")
    start(0, "dup", "ddown")
    got(1, "across")
    start(1, "dup", "ddown")
    got(0, "far0", "far1")
    start(0, "dfar")
    over_x(bz, bx)
    got(1, "far0", "far1")
    start(1, "dfar")
    project(xb.at[0], src[0])
    exchange_sum(u_part, u_in, u_blk, u_all, u_rs, u_ag)
    project(xb.at[1], src[1])
    project(xb.at[2], src[2])
    project(xb.at[3], src[3])
    for c in bx:
        c.wait_recv()
    unpack(fac_b, fb, 384)
    prepare()
    got(0, "dup", "ddown")
    got(1, "dup", "ddown")
    project(xb.at[4], src[4])
    project(xb.at[5], src[5])
    got(0, "dfar")
    got(1, "dfar")
    project(xb.at[6], src[6])
    for c in u_ag:
        c.wait_recv()
    both = pl.ds(0, ROWS)
    for h in range(2):
        activate(h)
        to_block(s2p, rows_half(h), fs(1, True))
        rstart(h, "t2p")
        to_block(s2m, rows_half(h), fs(3, True))
        rstart(h, "t2m")
        to_block(s1, rows_half(h), fs(2, True))
        rstart(h, "t1")
        if h == 1:
            rstart(1, "t6p", "t6m")
    v_part[...] = dot_nt(hid[...], bd_t[...]).astype(BF16)
    for i in far_first:
        v_rs[i].start()
    to_block(s3, both, fs(2, False))
    to_block(s4p, both, fs(1, False))
    to_block(s4m, both, fs(3, False))
    send_far(0)
    rstart(0, "t4p1", "t4m0")
    to_block(s5, both, fs(0, True))
    acc[:, 0:COLS] = block(both, f)
    send_across(0)
    send_far(1)
    rgot(1, "t6p", "t6m")
    last, lead = pl.ds(ROWS - SHIFT, SHIFT), pl.ds(HALF, SHIFT)
    s4p[last, :] = (s4p[last, :].astype(F32) + r6p[...].astype(F32)).astype(BF16)
    s4m[lead, :] = (s4m[lead, :].astype(F32) + r6m[...].astype(F32)).astype(BF16)
    rstart(1, "t4p1", "t4m0")
    send_near(0)
    exchange_sum(v_part, v_in, v_blk, v_all, v_rs, v_ag)
    send_across(1)
    send_near(1)
    for c in v_ag:
        c.wait_recv()
    acc[:, 0:COLS] += dot_nn(v_all[...], ad_c[...])
    finish(0)
    finish(1)
    for c in stores:
        c.wait()
    for c in az + ax + bz + bx + u_rs + u_ag + v_rs + v_ag:
        c.wait_send()
    for t in tok + red:
        for c in t.values():
            c.wait_send()


N_COPIES = 20 + 16 + 28 + 20 + 2 + 12


def per_device(tokens, norm_gain, route_ids, route_gates, w_gate, w_up, w_down, a_factors, b_factors):
    hbm = pl.BlockSpec(memory_space=pl.ANY)
    block = pltpu.VMEM((ROWS, COLS), BF16)
    return pl.pallas_call(
        body,
        out_shape=jax.ShapeDtypeStruct((ROWS, COLS), BF16),
        in_specs=[hbm] * 9,
        out_specs=hbm,
        scratch_shapes=[
            pltpu.VMEM((ROWS, COLS), BF16),
            pltpu.VMEM((1, WIDTH), F32),
            pltpu.VMEM((2, ROWS), jnp.int32),
            pltpu.VMEM((2, ROWS), F32),
            pltpu.VMEM((2, 3, 2, COLS), F32),
            pltpu.VMEM((2, 3, 2, HID), F32),
            pltpu.VMEM((4 * HID, WIDTH), BF16),
            pltpu.VMEM((2 * HID, WIDTH), BF16),
            pltpu.VMEM((8, 512), F32),
            pltpu.VMEM((8, 768), F32),
            pltpu.VMEM((4, 4, 2, 16, 256), BF16),
            pltpu.VMEM((4, 4, 2, 16, 384), BF16),
            pltpu.VMEM((256, 512), BF16),
            pltpu.VMEM((256, 768), BF16),
            pltpu.VMEM((256, 4 * HID), BF16),
            pltpu.VMEM((128, 2 * HID), BF16),
            pltpu.VMEM((128, COLS), BF16),
            pltpu.VMEM((ROWS, 2 * HID), F32),
            pltpu.VMEM((7, ROWS, COLS), BF16),
            pltpu.VMEM((ROWS, 4 * HID), F32),
            pltpu.VMEM((ROWS, 128), F32),
            pltpu.VMEM((ROWS, 2 * HID), BF16),
            pltpu.VMEM((ROWS, 256), BF16),
            pltpu.VMEM((7, UB, 256), BF16),
            pltpu.VMEM((UB, 256), BF16),
            pltpu.VMEM((ROWS, 256), BF16),
            pltpu.VMEM((ROWS, 128), BF16),
            pltpu.VMEM((7, UB, 128), BF16),
            pltpu.VMEM((UB, 128), BF16),
            pltpu.VMEM((ROWS, 128), BF16),
        ] + [block] * 15 + [
            pltpu.VMEM((SHIFT, COLS), BF16),
            pltpu.VMEM((SHIFT, COLS), BF16),
            pltpu.SemaphoreType.DMA((14,)),
            pltpu.SemaphoreType.DMA((N_COPIES,)),
            pltpu.SemaphoreType.DMA((N_COPIES,)),
        ],
        compiler_params=pltpu.CompilerParams(
            collective_id=0, has_side_effects=True, vmem_limit_bytes=60 * 2**20
        ),
    )(tokens, norm_gain.reshape(1, WIDTH), route_ids.T, route_gates.T, w_gate, w_up, w_down, a_factors, b_factors)


def solution(mesh):
    placed = (
        P("wide", "fsdp"),
        P(),
        P("wide", None),
        P("wide", None),
        P(None, "fsdp", None),
        P(None, "fsdp", None),
        P(None, "fsdp", None),
        P(None, None, "wide", "fsdp"),
        P(None, None, "wide", "fsdp"),
    )
    return jax.shard_map(
        per_device, mesh=mesh, in_specs=placed, out_specs=P("wide", "fsdp"), check_vma=False
    )
```

```python
import functools

import jax
import jax.numpy as jnp
from jax import lax
from jax.experimental import pallas as pl
from jax.experimental.pallas import tpu as pltpu
from jax.sharding import PartitionSpec as P

F32, BF16 = jnp.float32, jnp.bfloat16
MESH = pl.DeviceIdType.MESH
ROWS, COLS, HID, WIDTH = 256, 512, 192, 4096
HALF, QUART = 128, 64
UB = 32
SHIFT = 48


def dot_nt(a, b):
    return lax.dot_general(a, b, (((1,), (1,)), ((), ())), preferred_element_type=F32)


def dot_nn(a, b):
    return jnp.dot(a, b, preferred_element_type=F32)


def iota(shape, dim):
    return lax.broadcasted_iota(jnp.int32, shape, dim)


def body(
    x_hbm, gain_hbm, ids_hbm, gates_hbm, wg_hbm, wu_hbm, wd_hbm, a_hbm, b_hbm, out_hbm,
    x_ref, gain_ref, ids_ref, gates_ref, a_ref, b_ref, w_in, w_down, pack_a, pack_b, fac_a, fac_b, fa, fb, b_exp, bd_t, ad_c, mixed,
    xb, acc, sq, hid,
    u_part, u_in, u_blk, u_all, v_part, v_in, v_blk, v_all,
    s1, s2p, s2m, s3, s4p, s4m, s5, r1, r2p, r2m, r3, r4p, r4m, r5,
    o_buf, r6p, r6m, wsem, ssem, rsem,
):
    w = lax.axis_index("wide")
    f = lax.axis_index("fsdp")
    zh, xx, core = w // 8, (w // 2) % 4, w % 2
    y, z = f // 2, f % 2

    def fs(dy, flip):
        zz = 1 - z if flip else z
        return ((y + dy) % 4) * 2 + zz

    def wide_at(dzh, dx, dcore):
        return (((zh + dzh) % 4) * 4 + (xx + dx) % 4) * 2 + (core + dcore) % 2

    up, down, across = (w, fs(1, False)), (w, fs(3, False)), (w, fs(0, True))
    count = [0]

    def remote(src, dst, dev):
        i = count[0]
        count[0] += 1
        return pltpu.make_async_remote_copy(
            src_ref=src, dst_ref=dst, send_sem=ssem.at[i], recv_sem=rsem.at[i],
            device_id=dev, device_id_type=MESH,
        )

    small = [
        pltpu.make_async_copy(src, dst, wsem.at[6 + i])
        for i, (src, dst) in enumerate((
            (a_hbm, a_ref), (b_hbm, b_ref), (x_hbm, x_ref),
            (gain_hbm, gain_ref), (ids_hbm, ids_ref), (gates_hbm, gates_ref),
        ))
    ]
    small[0].start()

    peers = [(wide_at(d // 2, 0, d % 2), f) for d in range(1, 8)] + [(wide_at(0, d, 0), f) for d in (1, 2, 3)]
    peers += [(w, (f + i) % 8) for i in range(1, 8)]
    barrier = pltpu.get_barrier_semaphore()
    for p in peers:
        pl.semaphore_signal(barrier, inc=1, device_id=p, device_id_type=MESH)

    for c in small[1:]:
        c.start()
    loads = []
    for e in range(2):
        for j, (ref, dst) in enumerate(((wg_hbm, w_in.at[pl.ds(e * HID, HID)]),
                                        (wu_hbm, w_in.at[pl.ds((2 + e) * HID, HID)]),
                                        (wd_hbm, w_down.at[pl.ds(e * HID, HID)]))):
            c = pltpu.make_async_copy(ref.at[e], dst, wsem.at[e * 3 + j])
            c.start()
            loads.append(c)

    small[0].wait()
    for e in range(2):
        for p in range(2):
            pack_a[e * 4 + p * 2:e * 4 + p * 2 + 2, :] = a_ref[e, p]
    fac_a[0, 0, 0] = jnp.concatenate([pack_a[:, 0:256], pack_a[:, 256:512]], axis=0).astype(BF16)

    def pack_second():
        pack_b[...] = jnp.zeros_like(pack_b)
        for e in range(2):
            for p in range(2):
                pack_b[e * 4 + p * 2:e * 4 + p * 2 + 2, 0:192] = b_ref[e, p]
            for h in range(2):
                pack_b[h * 4 + e * 2:h * 4 + e * 2 + 2, 256:512] = a_ref[e, 2, :, h * 256:(h + 1) * 256]
            pack_b[e * 2:e * 2 + 2, 512:704] = b_ref[e, 2]
        fac_b[0, 0, 0] = jnp.concatenate([pack_b[:, 0:384], pack_b[:, 384:768]], axis=0).astype(BF16)

    pl.semaphore_wait(barrier, len(peers))

    def half(ref, h):
        return ref.at[pl.ds(h * HALF, HALF)]

    def quart(ref, h, q):
        return ref.at[pl.ds(h * HALF + q * QUART, QUART)]

    near = [(dz, dc) for dz in (2, 1, 3, 0) for dc in (0, 1) if dz or dc]

    def factor_copies(fac):
        by_z = [
            remote(fac.at[0, 0, 0], fac.at[0, (4 - dz) % 4, dc], (wide_at(dz, 0, dc), f)) for dz, dc in near
        ]
        by_x = [remote(fac.at[0], fac.at[4 - d], (wide_at(0, d, 0), f)) for d in (2, 1, 3)]
        return by_z, by_x

    az, _ = factor_copies(fac_a)
    ax_of = {
        slot: [remote(fac_a.at[0, slot], fac_a.at[4 - d, slot], (wide_at(0, d, 0), f)) for d in (2, 1, 3)]
        for slot in (0, 1, 3, 2)
    }
    ax = [c for slot in (0, 1, 3, 2) for c in ax_of[slot]]
    bz, bx = factor_copies(fac_b)
    tok = []
    for h in range(2):
        t = {}
        t["up"] = remote(half(x_ref, h), half(xb.at[0], h), up)
        t["down"] = remote(half(x_ref, h), half(xb.at[1], h), down)
        t["across"] = remote(half(x_ref, h), half(xb.at[2], h), across)
        t["far0"] = remote(quart(xb.at[0], h, 0), quart(xb.at[3], h, 0), up)
        t["far1"] = remote(quart(xb.at[1], h, 1), quart(xb.at[3], h, 1), down)
        t["dup"] = remote(half(xb.at[2], h), half(xb.at[4], h), up)
        t["ddown"] = remote(half(xb.at[2], h), half(xb.at[5], h), down)
        t["dfar"] = remote(half(xb.at[3], h), half(xb.at[6], h), across)
        tok.append(t)
    src = [fs(3, False), fs(1, False), fs(0, True), fs(2, False), fs(3, True), fs(1, True), fs(2, True)]
    other = [(w, (f + i) % 8) for i in range(1, 8)]
    mine = pl.ds(pl.multiple_of(f * UB, UB), UB)

    far_first = (2, 4, 3, 1, 5, 0, 6)

    def rows_of(i):
        return pl.ds(pl.multiple_of(((f + i) % 8) * UB, UB), UB)

    u_rs = [remote(u_part.at[rows_of(i)], u_in.at[i - 1], other[i - 1]) for i in range(1, 8)]
    u_ag = [remote(u_blk, u_all.at[mine], other[i - 1]) for i in range(1, 8)]
    v_rs = [remote(v_part.at[rows_of(i)], v_in.at[i - 1], other[i - 1]) for i in range(1, 8)]
    v_ag = [remote(v_blk, v_all.at[mine], other[i - 1]) for i in range(1, 8)]
    red = []
    for h in range(2):
        t = {}
        t["t1"] = remote(half(s1, h), half(r1, h), across)
        kept_p = pl.ds(h * HALF, HALF - h * SHIFT)
        kept_m = pl.ds(h * HALF + h * SHIFT, HALF - h * SHIFT)
        t["t2p"] = remote(s2p.at[kept_p], r2m.at[kept_p], up)
        t["t2m"] = remote(s2m.at[kept_m], r2p.at[kept_m], down)
        if h == 1:
            t["t6p"] = remote(s2p.at[pl.ds(ROWS - SHIFT, SHIFT)], r6p, across)
            t["t6m"] = remote(s2m.at[pl.ds(HALF, SHIFT)], r6m, across)
        t["t3p"] = remote(quart(s3, h, 0), quart(r3, h, 0), up)
        t["t3m"] = remote(quart(s3, h, 1), quart(r3, h, 1), down)
        t["t4p0"] = remote(quart(s4p, h, 0), quart(r4m, h, 0), up)
        t["t4p1"] = remote(quart(s4p, h, 1), quart(r4m, h, 1), up)
        t["t4m0"] = remote(quart(s4m, h, 0), quart(r4p, h, 0), down)
        t["t4m1"] = remote(quart(s4m, h, 1), quart(r4p, h, 1), down)
        t["t5"] = remote(half(s5, h), half(r5, h), across)
        red.append(t)

    def start(h, *names):
        for n in names:
            tok[h][n].start()

    def got(h, *names):
        for n in names:
            tok[h][n].wait_recv()

    def rstart(h, *names):
        for n in names:
            red[h][n].start()

    def rgot(h, *names):
        for n in names:
            red[h][n].wait_recv()

    def scaled(ref, owner):
        lanes = pl.ds(pl.multiple_of(owner * COLS, COLS), COLS)
        v = ref[...].astype(F32)
        s = v * v
        s = (s[:, 0:128] + s[:, 128:256]) + (s[:, 256:384] + s[:, 384:512])
        return (v * gain_ref[:, lanes]).astype(BF16), s, lanes

    def project(ref, owner, first=False):
        xg, s, lanes = scaled(ref, owner)
        prod = dot_nt(xg, w_in[:, lanes])
        if first:
            acc[...] = prod
            sq[...] = s
        else:
            acc[...] += prod
            sq[...] += s

    def block(rows, owner):
        lanes = pl.ds(pl.multiple_of(owner * COLS, COLS), COLS)
        return dot_nn(hid[rows, :], w_down[:, lanes])

    def activate(h):
        rows = pl.ds(h * HALF, HALF)
        mean = jnp.sum(sq[rows, :], axis=-1, keepdims=True) * (1.0 / WIDTH)
        scale = lax.rsqrt(mean + 1e-06)
        pre = (acc[rows, :] + dot_nn(u_all[rows, :], b_exp[...])) * scale
        g, u = pre[:, 0:2 * HID], pre[:, 2 * HID:4 * HID]
        hid[rows, :] = (g / (1.0 + jnp.exp(-g)) * u * mixed[rows, :]).astype(BF16)

    def mix_rows():
        ids, gates = ids_ref[...], gates_ref[...]
        mix = [jnp.sum(jnp.where(ids == e, gates, 0.0), axis=0, keepdims=True) for e in range(2)]
        r = iota((8, ROWS), 0)
        mix = jnp.where(r == 0, mix[0], jnp.where(r == 1, mix[1], 0.0))
        pick = (iota((8, 2 * HID), 0) == iota((8, 2 * HID), 1) // HID).astype(F32)
        mixed[...] = lax.dot_general(
            mix, pick, (((0,), (0,)), ((), ())), precision=lax.Precision.HIGHEST, preferred_element_type=F32
        )

    def to_block(dst, rows, owner):
        dst[rows, :] = block(rows, owner).astype(BF16)

    def rows_half(h):
        return pl.ds(h * HALF, HALF)

    def send_far(h):
        rows = rows_half(h)
        rgot(h, "t1")
        s3[rows, :] = (s3[rows, :].astype(F32) + r1[rows, :].astype(F32)).astype(BF16)
        rstart(h, "t3p", "t3m")

    def send_across(h):
        rows = rows_half(h)
        rgot(h, "t2p", "t2m")
        kept_p = pl.ds(h * HALF, HALF - h * SHIFT)
        kept_m = pl.ds(h * HALF + h * SHIFT, HALF - h * SHIFT)
        total = s5[rows, :].astype(F32)
        low, high = r2m[kept_p, :].astype(F32), r2p[kept_m, :].astype(F32)
        if h == 1:
            none = jnp.zeros((SHIFT, COLS), F32)
            low, high = jnp.concatenate([low, none], axis=0), jnp.concatenate([none, high], axis=0)
        s5[rows, :] = (total + low + high).astype(BF16)
        rstart(h, "t5")

    def send_near(h):
        q0, q1 = pl.ds(h * HALF, QUART), pl.ds(h * HALF + QUART, QUART)
        rgot(h, "t3p")
        s4p[q0, :] = (s4p[q0, :].astype(F32) + r3[q0, :].astype(F32)).astype(BF16)
        rstart(h, "t4p0")
        rgot(h, "t3m")
        s4m[q1, :] = (s4m[q1, :].astype(F32) + r3[q1, :].astype(F32)).astype(BF16)
        rstart(h, "t4m1")

    stores = [pltpu.make_async_copy(half(o_buf, h), half(out_hbm, h), wsem.at[12 + h]) for h in range(2)]

    def finish(h):
        rows = rows_half(h)
        rgot(h, "t5", "t4p1", "t4m0", "t4p0", "t4m1")
        part = acc[rows, 0:COLS] + r4p[rows, :].astype(F32) + r4m[rows, :].astype(F32) + r5[rows, :].astype(F32)
        o_buf[rows, :] = part.astype(BF16)
        stores[h].start()

    def exchange_sum(part, arrived, blk, whole, rs, ag):
        total = part[mine, :].astype(F32)
        for i in range(7):
            rs[i].wait_recv()
            total = total + arrived[i].astype(F32)
        blk[...] = total.astype(BF16)
        whole[mine, :] = total.astype(BF16)
        for i in far_first:
            ag[i].start()

    def over_x(by_z, by_x):
        for c in by_z:
            c.wait_recv()
        for c in by_x:
            c.start()

    def unpack(fac, whole, width):
        def step(i, carry):
            rows = pl.ds(pl.multiple_of(i * 16, 16), 16)
            two = [fac[i // 4, i % 4, k].astype(F32) for k in range(2)]
            whole[rows, 0:width] = jnp.concatenate([two[0][0:8], two[1][0:8]], axis=0).astype(BF16)
            whole[rows, width:2 * width] = jnp.concatenate([two[0][8:16], two[1][8:16]], axis=0).astype(BF16)
            return carry

        lax.fori_loop(0, 16, step, 0)

    def prepare():
        rep = (iota((256, 4 * HID), 0) == iota((256, 4 * HID), 1) % HID).astype(BF16)
        k, j = iota((256, 4 * HID), 0), iota((256, 4 * HID), 1) // HID
        keep = ((k % 8) // 4 + 2 * ((k % 4) // 2)) == j
        b_exp[...] = jnp.where(keep, 2.0 * dot_nn(fb[:, 0:256], rep), 0.0).astype(BF16)
        r, k = iota((128, 256), 0), iota((128, 256), 1)
        slot = (r // 4) * 8 + r % 4
        sel0, sel1 = (k == slot).astype(BF16), (k == slot + 4).astype(BF16)
        bd = dot_nn(sel0, fb[:, 512:768]).astype(BF16)
        r, j = iota((128, 2 * HID), 0), iota((128, 2 * HID), 1) // HID
        bd_t[...] = jnp.where((r % 4) // 2 == j, dot_nn(bd, rep[:, 0:2 * HID]), 0.0).astype(BF16)
        ad_c[:, 0:256] = (2.0 * dot_nn(sel0, fb[:, 256:512])).astype(BF16)
        ad_c[:, 256:512] = (2.0 * dot_nn(sel1, fb[:, 256:512])).astype(BF16)

    for c in az:
        c.start()
    for c in small[1:]:
        c.wait()
    start(0, "across", "up", "down")
    start(1, "across", "up", "down")
    pack_second()
    for c in loads:
        c.wait()
    project(x_ref, f, True)
    mix_rows()
    for slot in (0, 1, 3, 2):
        for c, (dz, dc) in zip(az, near):
            if (4 - dz) % 4 == slot:
                c.wait_recv()
        for c in ax_of[slot]:
            c.start()
    for c in bz:
        c.start()
    got(0, "up")
    start(0, "far0")
    got(0, "down")
    start(0, "far1")
    got(1, "up")
    start(1, "far0")
    got(1, "down")
    start(1, "far1")
    for c in ax:
        c.wait_recv()
    unpack(fac_a, fa, 256)
    xg, _, _ = scaled(x_ref, f)
    u_part[...] = dot_nt(xg, fa[...]).astype(BF16)
    for i in far_first:
        u_rs[i].start()
    got(0, "across")
    start(0, "dup", "ddown")
    got(1, "across")
    start(1, "dup", "ddown")
    got(0, "far0", "far1")
    start(0, "dfar")
    over_x(bz, bx)
    got(1, "far0", "far1")
    start(1, "dfar")
    project(xb.at[0], src[0])
    exchange_sum(u_part, u_in, u_blk, u_all, u_rs, u_ag)
    project(xb.at[1], src[1])
    project(xb.at[2], src[2])
    project(xb.at[3], src[3])
    for c in bx:
        c.wait_recv()
    unpack(fac_b, fb, 384)
    prepare()
    got(0, "dup", "ddown")
    got(1, "dup", "ddown")
    project(xb.at[4], src[4])
    project(xb.at[5], src[5])
    got(0, "dfar")
    got(1, "dfar")
    project(xb.at[6], src[6])
    for c in u_ag:
        c.wait_recv()
    both = pl.ds(0, ROWS)
    for h in range(2):
        activate(h)
        to_block(s2p, rows_half(h), fs(1, True))
        rstart(h, "t2p")
        to_block(s2m, rows_half(h), fs(3, True))
        rstart(h, "t2m")
        to_block(s1, rows_half(h), fs(2, True))
        rstart(h, "t1")
        if h == 1:
            rstart(1, "t6p", "t6m")
    v_part[...] = dot_nt(hid[...], bd_t[...]).astype(BF16)
    for i in far_first:
        v_rs[i].start()
    to_block(s3, both, fs(2, False))
    to_block(s4p, both, fs(1, False))
    to_block(s4m, both, fs(3, False))
    send_far(0)
    rstart(0, "t4p1", "t4m0")
    to_block(s5, both, fs(0, True))
    acc[:, 0:COLS] = block(both, f)
    send_across(0)
    send_far(1)
    rgot(1, "t6p", "t6m")
    last, lead = pl.ds(ROWS - SHIFT, SHIFT), pl.ds(HALF, SHIFT)
    s4p[last, :] = (s4p[last, :].astype(F32) + r6p[...].astype(F32)).astype(BF16)
    s4m[lead, :] = (s4m[lead, :].astype(F32) + r6m[...].astype(F32)).astype(BF16)
    rstart(1, "t4p1", "t4m0")
    send_near(0)
    exchange_sum(v_part, v_in, v_blk, v_all, v_rs, v_ag)
    send_across(1)
    send_near(1)
    for c in v_ag:
        c.wait_recv()
    acc[:, 0:COLS] += dot_nn(v_all[...], ad_c[...])
    finish(0)
    finish(1)
    for c in stores:
        c.wait()
    for c in az + ax + bz + bx + u_rs + u_ag + v_rs + v_ag:
        c.wait_send()
    for t in tok + red:
        for c in t.values():
            c.wait_send()


N_COPIES = 20 + 16 + 28 + 20 + 2 + 12


def per_device(tokens, norm_gain, route_ids, route_gates, w_gate, w_up, w_down, a_factors, b_factors):
    hbm = pl.BlockSpec(memory_space=pl.ANY)
    block = pltpu.VMEM((ROWS, COLS), BF16)
    return pl.pallas_call(
        body,
        out_shape=jax.ShapeDtypeStruct((ROWS, COLS), BF16),
        in_specs=[hbm] * 9,
        out_specs=hbm,
        scratch_shapes=[
            pltpu.VMEM((ROWS, COLS), BF16),
            pltpu.VMEM((1, WIDTH), F32),
            pltpu.VMEM((2, ROWS), jnp.int32),
            pltpu.VMEM((2, ROWS), F32),
            pltpu.VMEM((2, 3, 2, COLS), F32),
            pltpu.VMEM((2, 3, 2, HID), F32),
            pltpu.VMEM((4 * HID, WIDTH), BF16),
            pltpu.VMEM((2 * HID, WIDTH), BF16),
            pltpu.VMEM((8, 512), F32),
            pltpu.VMEM((8, 768), F32),
            pltpu.VMEM((4, 4, 2, 16, 256), BF16),
            pltpu.VMEM((4, 4, 2, 16, 384), BF16),
            pltpu.VMEM((256, 512), BF16),
            pltpu.VMEM((256, 768), BF16),
            pltpu.VMEM((256, 4 * HID), BF16),
            pltpu.VMEM((128, 2 * HID), BF16),
            pltpu.VMEM((128, COLS), BF16),
            pltpu.VMEM((ROWS, 2 * HID), F32),
            pltpu.VMEM((7, ROWS, COLS), BF16),
            pltpu.VMEM((ROWS, 4 * HID), F32),
            pltpu.VMEM((ROWS, 128), F32),
            pltpu.VMEM((ROWS, 2 * HID), BF16),
            pltpu.VMEM((ROWS, 256), BF16),
            pltpu.VMEM((7, UB, 256), BF16),
            pltpu.VMEM((UB, 256), BF16),
            pltpu.VMEM((ROWS, 256), BF16),
            pltpu.VMEM((ROWS, 128), BF16),
            pltpu.VMEM((7, UB, 128), BF16),
            pltpu.VMEM((UB, 128), BF16),
            pltpu.VMEM((ROWS, 128), BF16),
        ] + [block] * 15 + [
            pltpu.VMEM((SHIFT, COLS), BF16),
            pltpu.VMEM((SHIFT, COLS), BF16),
            pltpu.SemaphoreType.DMA((14,)),
            pltpu.SemaphoreType.DMA((N_COPIES,)),
            pltpu.SemaphoreType.DMA((N_COPIES,)),
        ],
        compiler_params=pltpu.CompilerParams(
            collective_id=0, has_side_effects=True, vmem_limit_bytes=60 * 2**20
        ),
    )(tokens, norm_gain.reshape(1, WIDTH), route_ids.T, route_gates.T, w_gate, w_up, w_down, a_factors, b_factors)


def solution(mesh):
    placed = (
        P("wide", "fsdp"),
        P(),
        P("wide", None),
        P("wide", None),
        P(None, "fsdp", None),
        P(None, "fsdp", None),
        P(None, "fsdp", None),
        P(None, None, "wide", "fsdp"),
        P(None, None, "wide", "fsdp"),
    )
    return jax.shard_map(
        per_device, mesh=mesh, in_specs=placed, out_specs=P("wide", "fsdp"), check_vma=False
    )
```
